32 devices in a mesh: rows: 8 (over z, x), tensor: 2 (over core), groups: 2 (over y).
Axes of the slice: x: 2, y: 2, z: 4, core: 2. Of those that a mesh axis runs over, the one named last changes fastest.
Arguments:
- effects: float32 [4096, 1024], P(('groups', 'rows'), 'tensor'), parts along dimension 0, may hold values from -8 to 8
Outputs:
- basis: float32 [4096, 1024], P(('groups', 'rows'), 'tensor'), parts along dimension 0
- triangle: float32 [2048, 1024], P('groups', 'tensor'), parts along dimension 0
The draws below stay inside these ranges and needn't reach their ends.
There are 2 independent parts, one for each index of `groups`. The reference program is written for one: setup_inputs(seed, part) draws one part's arguments, and reference() takes and returns one part's arrays. A program takes and returns all parts, laid end to end along the dimension named above; each array names one. Nothing has to cross between parts.
All inputs are finite; a program needn't handle non-finite values.
Results may differ from the reference program's by a relative error of at most 0.000075.
Values sent between devices are 32-bit elements; how exact they have to be, the bound alone decides.
No kernel may reach another device: no remote copies, remote signals or barrier semaphores. Data moves between devices by JAX's collectives and lax.ppermute only.
A program may use at most 64 MiB of HBM per device.

```python
import jax
import jax.numpy as jnp
from jax import lax

COLS = 1024
ROWS = 2048


def block_levels(rng, dims, split, smallest, largest):
    loudness = 1.0
    for axis_at, parts in split:
        steps = jax.random.uniform(jax.random.fold_in(jax.random.fold_in(rng, 6), axis_at), (parts,), jnp.float32, smallest / len(split), largest / len(split))
        loudness = loudness * jnp.repeat(jnp.exp(steps), dims[axis_at] // parts).reshape((-1,) + (1,) * (len(dims) - 1 - axis_at))
    return loudness


def gaussian(own_key, extent, deviation, reach, cuts=(), dtype=jnp.bfloat16):
    result = jax.random.normal(own_key, extent, jnp.float32) * deviation
    if len(cuts) > 0:
        result = block_levels(own_key, extent, cuts, -0.22, 0.18) * result
    return jnp.clip(result, min=-reach, max=reach).astype(dtype)


def setup_inputs(seed: int = 0, part: int = 0) -> dict:
    arg_keys = jax.random.split(jax.random.key(seed), 2)
    own_keys = jax.random.split(jax.random.fold_in(arg_keys[1], part), 2)
    return {
        "effects": gaussian(own_keys[0], (ROWS, COLS), 1.0, 8.0, ((0, 8), (1, 2)), jnp.float32),
    }


def reference(effects):
    gram = jnp.dot(effects.T.astype(jnp.float32), effects.astype(jnp.float32), precision=lax.Precision.HIGHEST, preferred_element_type=jnp.float32)
    lower = jnp.linalg.cholesky(gram)
    total = effects.shape[0]
    solved = lax.linalg.triangular_solve(lower, effects, left_side=False, lower=True, transpose_a=True)
    basis = solved * jnp.sqrt(jnp.float32(total))
    triangle = lower.T / jnp.sqrt(jnp.float32(total))
    return (basis, triangle)
```

```python
import functools

import jax
import jax.numpy as jnp
from jax import lax
from jax.experimental import pallas as pl
from jax.experimental.pallas import tpu as pltpu
from jax.sharding import PartitionSpec as P

F32 = jnp.float32
HIGHEST = lax.Precision.HIGHEST
NB = 128
SUB = 8


def dot(a, b, dims=((1,), (0,))):
    return lax.dot_general(a, b, (dims, ((), ())), precision=HIGHEST, preferred_element_type=F32)


def row_of(x, k):
    return jnp.broadcast_to(x[k : k + 1, :], x.shape)


def lane_of(x, j):
    return jnp.broadcast_to(x[:, j : j + 1], x.shape)


def factor_block(rows, put_upper, put_inverse):
    lane = lax.broadcasted_iota(jnp.int32, (SUB, NB), 1)
    sub = lax.broadcasted_iota(jnp.int32, (SUB, NB), 0)
    rows = list(rows)
    count = len(rows)
    for g in range(count):
        first = SUB * g
        raw = rows[g]
        cols = [lane_of(raw, first + k) for k in range(SUB)]
        below = {h: [lane_of(rows[h], first + k) for k in range(SUB)] for h in range(g + 1, count)}
        in_group = (lane >= first) & (lane < first + SUB)
        right = raw
        left = jnp.where(in_group, jnp.where(lane - first == sub, F32(1), F32(0)), raw)
        upper = jnp.zeros_like(raw)
        inverse = jnp.zeros_like(raw)
        for k in range(SUB):
            mine = sub == k
            pivot = row_of(cols[k], k)
            recip = 1.0 / pivot
            root = lax.rsqrt(pivot)
            right_k, left_k = row_of(right, k), row_of(left, k)
            upper = jnp.where(mine, right_k * root, upper)
            inverse = jnp.where(mine, left_k * root, inverse)

            def eliminate(x, x_k):
                scaled = x_k * recip
                return jnp.where(mine, scaled, x - cols[k] * scaled)

            for m in range(k + 1, SUB):
                cols[m] = eliminate(cols[m], row_of(cols[m], k))
            right, left = eliminate(right, right_k), eliminate(left, left_k)
        put_upper(g, jnp.where(lane >= sub + first, upper, F32(0)))
        put_inverse(g, jnp.where(lane <= sub + first, inverse, F32(0)))
        solved = jnp.where(lane < first + SUB, left, right)
        solved_rows = [row_of(solved, k) for k in range(SUB)]
        for h in range(g + 1, count):
            p = [below[h][k] * solved_rows[k] for k in range(SUB)]
            total = ((p[0] + p[1]) + (p[2] + p[3])) + ((p[4] + p[5]) + (p[6] + p[7]))
            rows[h] = jnp.where(in_group, F32(0), rows[h]) - total


def pairs(n):
    return [(i, j) for i in range(n) for j in range(i, n)]


def gram_diag_kernel(own_ref, out_ref):
    blocks = own_ref.shape[1] // NB
    for at, (i, j) in enumerate(pairs(blocks)):
        out_ref[at * NB : (at + 1) * NB, :] = dot(
            own_ref[:, i * NB : (i + 1) * NB], own_ref[:, j * NB : (j + 1) * NB], ((0,), (0,))
        )


def gram_cross_kernel(first_ref, second_ref, out_ref):
    for i in range(first_ref.shape[1] // NB):
        for j in range(second_ref.shape[1] // NB):
            at = i * (second_ref.shape[1] // NB) + j
            out_ref[at * NB : (at + 1) * NB, :] = dot(
                first_ref[:, i * NB : (i + 1) * NB], second_ref[:, j * NB : (j + 1) * NB], ((0,), (0,))
            )


def solve_kernel(scale, t_ref, pay0_ref, pay1_ref, e0_ref, e1_ref, basis_ref, tri_ref, a_ref, e_ref, inv_ref):
    width = e0_ref.shape[1]
    half = width // NB
    n = 2 * half
    diag = pairs(half)

    def block(r, c):
        return slice(r * NB, (r + 1) * NB), slice(c * NB, (c + 1) * NB)

    for at, (i, j) in enumerate(diag):
        a_ref[block(i, j)] = pay0_ref[at * NB : (at + 1) * NB, :]
        a_ref[block(half + i, half + j)] = pay1_ref[at * NB : (at + 1) * NB, :]
    at = len(diag)
    for i in range(half):
        for j in range(half // 2):
            piece = slice(at * NB, (at + 1) * NB)
            a_ref[block(i, half + j)] = pay0_ref[piece, :]
            a_ref[block(i, half + half // 2 + j)] = pay1_ref[piece, :]
            at += 1
    e_ref[:, :width] = e0_ref[...]
    e_ref[:, width:] = e1_ref[...]

    for k in range(n):
        here = slice(k * NB, (k + 1) * NB)
        rest = slice((k + 1) * NB, n * NB)
        rows = [a_ref[k * NB + SUB * h : k * NB + SUB * (h + 1), here] for h in range(NB // SUB)]

        def put_upper(g, v):
            a_ref[k * NB + SUB * g : k * NB + SUB * (g + 1), here] = v

        def put_inverse(g, v):
            inv_ref[SUB * g : SUB * (g + 1), :] = v

        factor_block(rows, put_upper, put_inverse)
        inverse = inv_ref[...]
        solved = dot(e_ref[:, here], inverse.T)
        e_ref[:, here] = solved
        if k + 1 < n:
            upper = dot(inverse, a_ref[here, rest])
            a_ref[here, rest] = upper
            lower = upper.T
            for i in range(k + 1, n):
                off = (i - k - 1) * NB
                cols = slice(i * NB, n * NB)
                a_ref[i * NB : (i + 1) * NB, cols] -= dot(lower[off : off + NB, :], upper[:, off:])
            e_ref[:, rest] -= dot(solved, upper)

    start = pl.multiple_of(t_ref[0] * width, NB)
    basis_ref[...] = e_ref[:, pl.ds(start, width)] * scale
    for r in range(n):
        for c in range(half):
            col = t_ref[0] * half + c
            value = a_ref[r * NB : (r + 1) * NB, pl.ds(pl.multiple_of(col * NB, NB), NB)]
            tri_ref[r * NB : (r + 1) * NB, c * NB : (c + 1) * NB] = jnp.where(r <= col, value / scale, F32(0))


def sum_rows(payload, n):
    me = lax.axis_index("rows")
    parity, far = me % 2, me // 2
    nfar = n // 2
    size = payload.shape[0] // 2
    piece = size // nfar
    pair = [(i, i ^ 1) for i in range(n)]
    keep = lax.dynamic_slice_in_dim(payload, parity * size, size)
    send = lax.dynamic_slice_in_dim(payload, (1 - parity) * size, size)
    mine = keep + lax.ppermute(send, "rows", pair)

    def to(s):
        return [(i, 2 * ((i // 2) ^ s) + i % 2) for i in range(n)]

    total = lax.dynamic_slice_in_dim(mine, far * piece, piece)
    for s in range(1, nfar):
        part = lax.dynamic_slice_in_dim(mine, (far ^ s) * piece, piece)
        total = total + lax.ppermute(part, "rows", to(s))
    gathered = jnp.zeros_like(mine)
    gathered = lax.dynamic_update_slice_in_dim(gathered, total, far * piece, 0)
    for s in range(1, nfar):
        gathered = lax.dynamic_update_slice_in_dim(gathered, lax.ppermute(total, "rows", to(s)), (far ^ s) * piece, 0)
    other = lax.ppermute(gathered, "rows", pair)
    first = jnp.where(parity == 0, gathered, other)
    second = jnp.where(parity == 0, other, gathered)
    return jnp.concatenate([first, second])


def shards(n_rows, effects):
    rows, width = effects.shape
    cols = 2 * width
    half = width // NB
    n_diag, n_cross = half * (half + 1) // 2, half * half // 2
    t = lax.axis_index("tensor")
    swap = [(0, 1), (1, 0)]
    other = lax.ppermute(effects, "tensor", swap)
    diag = pl.pallas_call(
        gram_diag_kernel,
        out_shape=jax.ShapeDtypeStruct((n_diag * NB, NB), F32),
        cost_estimate=pl.CostEstimate(flops=12 * rows * n_diag * NB * NB, bytes_accessed=4 * rows * width, transcendentals=0),
        name="gram_diag",
    )(effects)
    e0 = jnp.where(t == 0, effects, other)
    e1 = jnp.where(t == 0, other, effects)
    cross = pl.pallas_call(
        gram_cross_kernel,
        out_shape=jax.ShapeDtypeStruct((n_cross * NB, NB), F32),
        name="gram_cross",
    )(e0, lax.dynamic_slice_in_dim(e1, t * (width // 2), width // 2, 1))
    payload = sum_rows(jnp.concatenate([diag, cross]), n_rows)
    payload_other = lax.ppermute(payload, "tensor", swap)
    pay0 = jnp.where(t == 0, payload, payload_other)
    pay1 = jnp.where(t == 0, payload_other, payload)
    scale = float(rows * n_rows) ** 0.5
    vmem = pl.BlockSpec(memory_space=pltpu.VMEM)
    return pl.pallas_call(
        functools.partial(solve_kernel, scale),
        out_shape=(jax.ShapeDtypeStruct((rows, width), F32), jax.ShapeDtypeStruct((cols, width), F32)),
        in_specs=[pl.BlockSpec(memory_space=pltpu.SMEM)] + [vmem] * 4,
        out_specs=(vmem, vmem),
        scratch_shapes=[pltpu.VMEM((cols, cols), F32), pltpu.VMEM((rows, cols), F32), pltpu.VMEM((NB, NB), F32)],
        compiler_params=pltpu.CompilerParams(vmem_limit_bytes=48 * 2**20),
        name="cholesky_solve",
    )(t.reshape(1).astype(jnp.int32), pay0, pay1, e0, e1)


def solution(mesh):
    spec = P(("groups", "rows"), "tensor")
    return jax.shard_map(
        functools.partial(shards, mesh.shape["rows"]),
        mesh=mesh,
        in_specs=(spec,),
        out_specs=(spec, P("groups", "tensor")),
        check_vma=False,
    )
```

```python
import functools

import jax
import jax.numpy as jnp
from jax import lax
from jax.experimental import pallas as pl
from jax.experimental.pallas import tpu as pltpu
from jax.sharding import PartitionSpec as P

F32 = jnp.float32
BF16 = jnp.bfloat16
NB = 128
SUB = 8
PANEL = 4


def split(x):
    high = x.astype(BF16)
    rest = x - high.astype(F32)
    mid = rest.astype(BF16)
    return high, mid, (rest - mid.astype(F32)).astype(BF16)


def left_parts(x):
    h, m, l = split(x)
    return jnp.concatenate([h, h, m, m, h, l], axis=1)


def right_parts(x):
    h, m, l = split(x)
    return jnp.concatenate([h, m, h, m, l, h], axis=0)


def product(left, right):
    return jnp.dot(left, right, preferred_element_type=F32)


def row_of(x, k):
    return jnp.broadcast_to(x[k : k + 1, :], x.shape)


def lane_of(x, j):
    return jnp.broadcast_to(x[:, j : j + 1], x.shape)


def total_of(terms):
    terms = list(terms)
    while len(terms) > 1:
        terms = [terms[i] + terms[i + 1] if i + 1 < len(terms) else terms[i] for i in range(0, len(terms), 2)]
    return terms[0]


def factor_block(rows, put_upper, put_inverse):
    lane = lax.broadcasted_iota(jnp.int32, (SUB, NB), 1)
    sub = lax.broadcasted_iota(jnp.int32, (SUB, NB), 0)
    mine = [sub == k for k in range(SUB)]
    zero = jnp.zeros((SUB, NB), F32)
    rows = list(rows)
    count = len(rows)
    for p in range(0, count, PANEL):
        for g in range(p, p + PANEL, 2):
            b = SUB * g
            col0 = [lane_of(rows[g], b + k) for k in range(SUB)]
            col1 = [lane_of(rows[g + 1], b + k) for k in range(2 * SUB)]
            others = list(range(g + 2, p + PANEL)) + list(range(p, g))
            factors = {h: [lane_of(rows[h], b + k) for k in range(2 * SUB)] for h in others}
            group = (lane >= b) & (lane < b + 2 * SUB)
            a0, a1 = rows[g], rows[g + 1]
            w0 = jnp.where(group, jnp.where(lane - b == sub, F32(1), F32(0)), a0)
            w1 = jnp.where(group, jnp.where(lane - b - SUB == sub, F32(1), F32(0)), a1)

            pivots, upper, inverse = zero, a0, w0
            for k in range(SUB):
                pivot = row_of(col0[k], k)
                recip = 1.0 / pivot
                c0 = jnp.where(mine[k], F32(0), col0[k]) * recip
                c1 = col1[k] * recip
                pivots = jnp.where(mine[k], pivot, pivots)
                upper = jnp.where(mine[k], a0, upper)
                inverse = jnp.where(mine[k], w0, inverse)
                for m in range(k + 1, SUB):
                    s = row_of(col0[m], k)
                    col0[m] = col0[m] - c0 * s
                    col1[m] = col1[m] - c1 * s
                for m in range(SUB):
                    col1[SUB + m] = col1[SUB + m] - c1 * row_of(col1[k], m)
                a, w = row_of(a0, k), row_of(w0, k)
                a0, a1, w0, w1 = a0 - c0 * a, a1 - c1 * a, w0 - c0 * w, w1 - c1 * w
            recips, roots = 1.0 / pivots, lax.rsqrt(pivots)
            put_upper(g, jnp.where(lane >= sub + b, upper * roots, F32(0)))
            put_inverse(g, jnp.where(lane <= sub + b, inverse * roots, F32(0)))
            a0, w0 = a0 * recips, w0 * recips
            above = [lane_of(a0, b + SUB + k) for k in range(SUB)]

            pivots, upper, inverse = zero, a1, w1
            for k in range(SUB):
                pivot = row_of(col1[SUB + k], k)
                recip = 1.0 / pivot
                c1 = jnp.where(mine[k], F32(0), col1[SUB + k]) * recip
                pivots = jnp.where(mine[k], pivot, pivots)
                upper = jnp.where(mine[k], a1, upper)
                inverse = jnp.where(mine[k], w1, inverse)
                for m in range(k + 1, SUB):
                    col1[SUB + m] = col1[SUB + m] - c1 * row_of(col1[SUB + m], k)
                a1, w1 = a1 - c1 * row_of(a1, k), w1 - c1 * row_of(w1, k)
            recips, roots = 1.0 / pivots, lax.rsqrt(pivots)
            put_upper(g + 1, jnp.where(lane >= sub + b + SUB, upper * roots, F32(0)))
            put_inverse(g + 1, jnp.where(lane <= sub + b + SUB, inverse * roots, F32(0)))

            left = lane < b + 2 * SUB
            solved1 = jnp.where(left, w1, a1) * recips
            solved0 = jnp.where(left, w0, a0)
            lower_rows = [row_of(solved1, k) for k in range(SUB)]
            solved0 = solved0 - total_of(above[k] * lower_rows[k] for k in range(SUB))
            solved = [row_of(solved0, k) for k in range(SUB)] + lower_rows
            rows[g], rows[g + 1] = solved0, solved1
            for h in others:
                rows[h] = jnp.where(group, F32(0), rows[h]) - total_of(f * s for f, s in zip(factors[h], solved))
        end = p + PANEL
        if end < count:
            panel = jnp.concatenate([rows[h] if p <= h < end else zero for h in range(count)], axis=0)
            below = jnp.concatenate(rows[end:], axis=0)
            lanes = lax.broadcasted_iota(jnp.int32, below.shape, 1)
            in_panel = (lanes >= SUB * p) & (lanes < SUB * end)
            below = jnp.where(in_panel, F32(0), below) - product(left_parts(below), right_parts(panel))
            for i in range(end, count):
                rows[i] = below[SUB * (i - end) : SUB * (i - end + 1), :]


def pairs(n):
    return [(i, j) for i in range(n) for j in range(i, n)]


def at(i, size=NB):
    return slice(i * size, (i + 1) * size)


def gram_diag_kernel(own_ref, out_ref):
    n = own_ref.shape[1] // NB
    right = right_parts(own_ref[...])
    done = 0
    for i in range(n):
        row = product(left_parts(own_ref[:, at(i)].T), right[:, i * NB :])
        for j in range(n - i):
            out_ref[at(done), :] = row[:, at(j)]
            done += 1


def gram_cross_kernel(s_ref, diag_ref, own_ref, other_ref, keep_ref, send_ref, first_ref, second_ref, all_ref):
    width = own_ref.shape[1]
    half = width // 2

    @pl.when(s_ref[0] == 0)
    def _():
        first_ref[...] = own_ref[...]
        second_ref[...] = other_ref[:, :half]

    @pl.when(s_ref[0] != 0)
    def _():
        first_ref[...] = other_ref[...]
        second_ref[...] = own_ref[:, half:]

    done = diag_ref.shape[0] // NB
    all_ref[: done * NB, :] = diag_ref[...]
    right = right_parts(second_ref[...])
    for i in range(width // NB):
        row = product(left_parts(first_ref[:, at(i)].T), right)
        for j in range(half // NB):
            all_ref[at(done), :] = row[:, at(j)]
            done += 1
    size = keep_ref.shape[0]
    keep_ref[...] = all_ref[pl.ds(pl.multiple_of(s_ref[1] * size, SUB), size), :]
    send_ref[...] = all_ref[pl.ds(pl.multiple_of((1 - s_ref[1]) * size, SUB), size), :]


def solve_kernel(
    scale, s_ref, mine_a, mine_b, sib_a, sib_b, own_ref, other_ref, basis_ref, tri_ref, pay_ref, a_ref, e_ref, inv_ref
):
    width = own_ref.shape[1]
    half = width // NB
    n = 2 * half
    size = mine_a.shape[0]
    t = s_ref[0]

    def put(core, bit, ref):
        pay_ref[core, pl.ds(pl.multiple_of(bit * size, SUB), size), :] = ref[...]

    put(t, s_ref[1], mine_a)
    put(t, 1 - s_ref[1], mine_b)
    put(1 - t, s_ref[2], sib_a)
    put(1 - t, 1 - s_ref[2], sib_b)
    e_ref[:, pl.ds(pl.multiple_of(t * width, NB), width)] = own_ref[...]
    e_ref[:, pl.ds(pl.multiple_of((1 - t) * width, NB), width)] = other_ref[...]

    where = {}
    for number, (i, j) in enumerate(pairs(half)):
        where[i, j] = (0, number)
        where[half + i, half + j] = (1, number)
    number = len(pairs(half))
    for i in range(half):
        for j in range(half // 2):
            where[i, half + j] = (0, number)
            where[i, half + half // 2 + j] = (1, number)
            number += 1

    def gram(i, j):
        core, number = where[i, j]
        return pay_ref[core, at(number), :]

    for k in range(n):
        here = at(k)
        source = gram(k, k) if k == 0 else a_ref[here, here]
        rows = [source[at(h, SUB), :] for h in range(NB // SUB)]

        def put_upper(g, v):
            a_ref[k * NB + SUB * g : k * NB + SUB * (g + 1), here] = v

        def put_inverse(g, v):
            inv_ref[at(g, SUB), :] = v

        factor_block(rows, put_upper, put_inverse)
        if k:
            a_ref[here, : k * NB] = jnp.zeros((NB, k * NB), F32)
        inverse = inv_ref[...]
        inverse_left = left_parts(inverse)
        solved = product(left_parts(e_ref[:, here]), right_parts(inverse.T))
        if k + 1 < n:
            rest = slice((k + 1) * NB, n * NB)
            uppers, lowers, rights = {}, {}, {}
            for j in range(k + 1, n):
                uppers[j] = product(inverse_left, right_parts(gram(k, j) if k == 0 else a_ref[here, at(j)]))
                lowers[j] = left_parts(uppers[j].T)
                rights[j] = right_parts(uppers[j])
                a_ref[here, at(j)] = uppers[j]
            for i in range(k + 1, n):
                right = jnp.concatenate([rights[j] for j in range(i, n)], axis=1)
                update = product(lowers[i], right)
                for j in range(i, n):
                    old = gram(i, j) if k == 0 else a_ref[at(i), at(j)]
                    a_ref[at(i), at(j)] = old - update[:, at(j - i)]
            e_ref[:, rest] -= product(left_parts(solved), jnp.concatenate([rights[j] for j in range(k + 1, n)], axis=1))
        e_ref[:, here] = solved * scale
        tri_ref[here, :] = a_ref[here, pl.ds(pl.multiple_of(t * width, NB), width)] * (1.0 / scale)

    basis_ref[...] = e_ref[:, pl.ds(pl.multiple_of(t * width, NB), width)]


def shards(n_rows, effects):
    rows, width = effects.shape
    cols = 2 * width
    half = width // NB
    n_diag, n_cross = half * (half + 1) // 2, half * half // 2
    size = (n_diag + n_cross) * NB // 2
    t = lax.axis_index("tensor")
    me = lax.axis_index("rows")
    swap = [(0, 1), (1, 0)]

    steps = n_rows.bit_length() - 1
    masks = [[1 << j for j in range(steps)] for _ in range(2)]
    if steps > 1:
        masks[1][0], masks[1][1] = masks[1][1], masks[1][0]

    def exchange(x, j):
        perm = [(2 * r + c, 2 * (r ^ masks[c][j]) + c) for r in range(n_rows) for c in range(2)]
        return lax.ppermute(x, ("rows", "tensor"), perm)

    def bit(j, core):
        return jnp.where(core == 0, (me // masks[0][j]) % 2, (me // masks[1][j]) % 2)

    vmem = pl.BlockSpec(memory_space=pltpu.VMEM)
    smem = pl.BlockSpec(memory_space=pltpu.SMEM)
    params = pltpu.CompilerParams(vmem_limit_bytes=48 * 2**20)
    scalars = jnp.stack([t, bit(0, t), bit(0, 1 - t)]).astype(jnp.int32)

    other = lax.ppermute(effects, "tensor", swap)
    diag = pl.pallas_call(
        gram_diag_kernel,
        out_shape=jax.ShapeDtypeStruct((n_diag * NB, NB), F32),
        cost_estimate=pl.CostEstimate(flops=12 * rows * n_diag * NB * NB, bytes_accessed=4 * rows * width, transcendentals=0),
        compiler_params=params,
        name="gram_diag",
    )(effects)
    part = jax.ShapeDtypeStruct((size, NB), F32)
    keep, send = pl.pallas_call(
        gram_cross_kernel,
        out_shape=(part, part),
        in_specs=[smem, vmem, vmem, vmem],
        out_specs=(vmem, vmem),
        scratch_shapes=[pltpu.VMEM((rows, width), F32), pltpu.VMEM((rows, width // 2), F32), pltpu.VMEM((2 * size, NB), F32)],
        compiler_params=params,
        name="gram_cross",
    )(scalars, diag, effects, other)

    total = keep + exchange(send, 0)
    for j in range(1, steps):
        piece = total.shape[0] // 2
        v = bit(j, t)
        sent = lax.dynamic_slice_in_dim(total, (1 - v) * piece, piece)
        total = lax.dynamic_slice_in_dim(total, v * piece, piece) + exchange(sent, j)
    for j in range(steps - 1, 0, -1):
        got = exchange(total, j)
        v = bit(j, t)
        total = jnp.concatenate([jnp.where(v == 0, total, got), jnp.where(v == 0, got, total)])
    mine_b = exchange(total, 0)
    sib_a = lax.ppermute(total, "tensor", swap)
    sib_b = lax.ppermute(mine_b, "tensor", swap)

    scale = float(rows * n_rows) ** 0.5
    return pl.pallas_call(
        functools.partial(solve_kernel, scale),
        out_shape=(jax.ShapeDtypeStruct((rows, width), F32), jax.ShapeDtypeStruct((cols, width), F32)),
        in_specs=[smem] + [vmem] * 6,
        out_specs=(vmem, vmem),
        scratch_shapes=[
            pltpu.VMEM((2, 2 * size, NB), F32),
            pltpu.VMEM((cols, cols), F32),
            pltpu.VMEM((rows, cols), F32),
            pltpu.VMEM((NB, NB), F32),
        ],
        compiler_params=params,
        name="cholesky_solve",
    )(scalars, total, mine_b, sib_a, sib_b, effects, other)


def solution(mesh):
    spec = P(("groups", "rows"), "tensor")
    return jax.shard_map(
        functools.partial(shards, mesh.shape["rows"]),
        mesh=mesh,
        in_specs=(spec,),
        out_specs=(spec, P("groups", "tensor")),
        check_vma=False,
    )
```

```python
import functools

import jax
import jax.numpy as jnp
from jax import lax
from jax.experimental import pallas as pl
from jax.experimental.pallas import tpu as pltpu
from jax.sharding import PartitionSpec as P

F32 = jnp.float32
BF16 = jnp.bfloat16
NB = 128
SUB = 8


def split(x):
    high = x.astype(BF16)
    rest = x - high.astype(F32)
    mid = rest.astype(BF16)
    return high, mid, (rest - mid.astype(F32)).astype(BF16)


def left_parts(x):
    h, m, l = split(x)
    return jnp.concatenate([h, h, m, m, h, l], axis=1)


def right_parts(x):
    h, m, l = split(x)
    return jnp.concatenate([h, m, h, m, l, h], axis=0)


def product(left, right):
    return jnp.dot(left, right, preferred_element_type=F32)


def row_of(x, k):
    return jnp.broadcast_to(x[k : k + 1, :], x.shape)


def lane_of(x, j):
    return jnp.broadcast_to(x[:, j : j + 1], x.shape)


def total_of(terms):
    terms = list(terms)
    while len(terms) > 1:
        terms = [terms[i] + terms[i + 1] if i + 1 < len(terms) else terms[i] for i in range(0, len(terms), 2)]
    return terms[0]


def eliminate(cols, below, parts, mine):
    zero = jnp.zeros_like(cols[0])
    pivots = zero
    taken = [x[0] for x in parts]
    for k in range(0, SUB, 2):
        a, b, e = row_of(cols[k], k), row_of(cols[k], k + 1), row_of(cols[k + 1], k + 1)
        det = a * e - b * b
        recip = 1.0 / a
        second = a * (1.0 / det)
        ratio = b * recip
        first_of = [jnp.where(mine[k], zero, cols[k]) * recip]
        last = jnp.where(mine[k], b, jnp.where(mine[k + 1], zero, cols[k + 1] - cols[k] * ratio))
        second_of = [last * second]
        if below is not None:
            reduced = below[k + 1] - below[k] * ratio
            first_of.append(below[k] * recip)
            second_of.append(reduced * second)
        pivots = jnp.where(mine[k], a, jnp.where(mine[k + 1], e - b * ratio, pivots))
        for m in range(k + 2, SUB):
            u = row_of(cols[m], k)
            w = row_of(cols[m], k + 1) - ratio * u
            cols[m] = cols[m] - first_of[0] * u - second_of[0] * w
            if below is not None:
                below[m] = below[m] - first_of[1] * u - second_of[1] * w
        if below is not None:
            for m in range(SUB):
                change = first_of[1] * row_of(below[k], m) + second_of[1] * row_of(reduced, m)
                below[SUB + m] = below[SUB + m] - change
        for i, x in enumerate(parts):
            u = row_of(x[0], k)
            w = row_of(x[0], k + 1) - ratio * u
            taken[i] = jnp.where(mine[k], x[0], jnp.where(mine[k + 1], w, taken[i]))
            for v in range(len(x)):
                x[v] = x[v] - first_of[v] * u - second_of[v] * w
    return pivots, taken


def factor_block(rows, put_upper, put_inverse):
    lane = lax.broadcasted_iota(jnp.int32, (SUB, NB), 1)
    sub = lax.broadcasted_iota(jnp.int32, (SUB, NB), 0)
    mine = [sub == k for k in range(SUB)]
    zero = jnp.zeros((SUB, NB), F32)
    rows = list(rows)
    count = len(rows)

    def emit(g, pivots, upper, inverse):
        root = lax.rsqrt(pivots)
        put_upper(g, jnp.where(lane >= sub + SUB * g, upper * root, zero))
        put_inverse(g, jnp.where(lane <= sub + SUB * g, inverse * root, zero))

    for g in range(0, count, 2):
        b = SUB * g
        col0 = [lane_of(rows[g], b + k) for k in range(SUB)]
        col1 = [lane_of(rows[g + 1], b + k) for k in range(2 * SUB)]
        near = range(g + 2, min(count, g + 4))
        factors = {h: [lane_of(rows[h], b + k) for k in range(2 * SUB)] for h in near}
        group = (lane >= b) & (lane < b + 2 * SUB)
        a = [rows[g], rows[g + 1]]
        w = [
            jnp.where(group, jnp.where(lane - b == sub, F32(1), zero), a[0]),
            jnp.where(group, jnp.where(lane - b - SUB == sub, F32(1), zero), a[1]),
        ]
        pivots, taken = eliminate(col0, col1, [a, w], mine)
        emit(g, pivots, *taken)
        recips = 1.0 / pivots
        a0, w0 = a[0] * recips, w[0] * recips
        above = [lane_of(a0, b + SUB + k) for k in range(SUB)]
        a, w = [a[1]], [w[1]]
        pivots, taken = eliminate(col1[SUB:], None, [a, w], mine)
        emit(g + 1, pivots, *taken)

        left = lane < b + 2 * SUB
        solved1 = jnp.where(left, w[0], a[0]) * (1.0 / pivots)
        lower_rows = [row_of(solved1, k) for k in range(SUB)]
        solved0 = jnp.where(left, w0, a0) - total_of(c * r for c, r in zip(above, lower_rows))
        solved = [row_of(solved0, k) for k in range(SUB)] + lower_rows
        rows[g], rows[g + 1] = solved0, solved1
        for h in near:
            rows[h] = jnp.where(group, zero, rows[h]) - total_of(f * s for f, s in zip(factors[h], solved))
        far = g + 4
        if far < count:
            panel = jnp.concatenate([rows[h] if g <= h < g + 2 else zero for h in range(count)], axis=0)
            rest = jnp.concatenate(rows[far:], axis=0)
            lanes = lax.broadcasted_iota(jnp.int32, rest.shape, 1)
            in_group = (lanes >= b) & (lanes < b + 2 * SUB)
            rest = jnp.where(in_group, F32(0), rest) - product(left_parts(rest), right_parts(panel))
            for i in range(far, count):
                rows[i] = rest[SUB * (i - far) : SUB * (i - far + 1), :]


def at(i, size=NB):
    return slice(i * size, (i + 1) * size)


def apart(n):
    return [(i, j) for i in range(n) for j in range(i + 1, n)]


def triangle_masks():
    r = lax.broadcasted_iota(jnp.int32, (NB, NB), 0)
    c = lax.broadcasted_iota(jnp.int32, (NB, NB), 1)
    return r < c, r == c


def halves(bit, all_ref, keep_ref, send_ref):
    size = keep_ref.shape[0]
    keep_ref[...] = all_ref[pl.ds(pl.multiple_of(bit * size, SUB), size), :]
    send_ref[...] = all_ref[pl.ds(pl.multiple_of((1 - bit) * size, SUB), size), :]


def gram_diag_kernel(s_ref, own_ref, keep_ref, send_ref, all_ref):
    n = own_ref.shape[1] // NB
    right = right_parts(own_ref[...])
    rows = [product(left_parts(own_ref[:, at(i)].T), right[:, i * NB :]) for i in range(n)]
    above, on = triangle_masks()
    tail = (n // 2 + len(apart(n))) * NB
    all_ref[tail:, :] = jnp.zeros((all_ref.shape[0] - tail, NB), F32)
    for i in range(0, n, 2):
        first, second = rows[i][:, :NB], rows[i + 1][:, :NB]
        all_ref[at(i // 2), :] = jnp.where(above | on, first, second)
        all_ref[tail + i // 2 : tail + i // 2 + 1, :] = jnp.sum(jnp.where(on, second, F32(0)), axis=0, keepdims=True)
    for number, (i, j) in enumerate(apart(n)):
        all_ref[at(n // 2 + number), :] = rows[i][:, at(j - i)]
    halves(s_ref[1], all_ref, keep_ref, send_ref)


def gram_cross_kernel(s_ref, own_ref, other_ref, keep_ref, send_ref, first_ref, second_ref, all_ref):
    width = own_ref.shape[1]
    half = width // 2

    @pl.when(s_ref[0] == 0)
    def _():
        first_ref[...] = own_ref[...]
        second_ref[...] = other_ref[:, :half]

    @pl.when(s_ref[0] != 0)
    def _():
        first_ref[...] = other_ref[...]
        second_ref[...] = own_ref[:, half:]

    right = right_parts(second_ref[...])
    per_row = half // NB
    for i in range(width // NB):
        row = product(left_parts(first_ref[:, at(i)].T), right)
        for j in range(per_row):
            all_ref[at(i * per_row + j), :] = row[:, at(j)]
    halves(s_ref[3], all_ref, keep_ref, send_ref)


def solve_kernel(scale, s_ref, *refs):
    sums, (own_ref, other_ref, basis_ref, tri_ref, diag_ref, cross_ref, a_ref, e_ref, inv_ref) = refs[:8], refs[8:]
    width = own_ref.shape[1]
    half = width // NB
    n = 2 * half
    t = s_ref[0]

    for pay_ref, parts, bit in ((diag_ref, sums[:4], 1), (cross_ref, sums[4:], 3)):
        size = parts[0].shape[0]
        places = ((t, s_ref[bit]), (t, 1 - s_ref[bit]), (1 - t, s_ref[bit + 1]), (1 - t, 1 - s_ref[bit + 1]))
        for (core, which), ref in zip(places, parts):
            pay_ref[core, pl.ds(pl.multiple_of(which * size, SUB), size), :] = ref[...]
    e_ref[:, pl.ds(pl.multiple_of(t * width, NB), width)] = own_ref[...]
    e_ref[:, pl.ds(pl.multiple_of((1 - t) * width, NB), width)] = other_ref[...]

    above, on = triangle_masks()
    tail = (half // 2 + len(apart(half))) * NB
    number_of = {ij: half // 2 + number for number, ij in enumerate(apart(half))}

    def gram(i, j):
        if i < half <= j:
            core, col = divmod(j - half, half // 2)
            return cross_ref[core, at(i * (half // 2) + col), :]
        core, i, j = i // half, i % half, j % half
        if i != j:
            return diag_ref[core, at(number_of[i, j]), :]
        both = diag_ref[core, at(i // 2), :]
        if i % 2 == 0:
            return jnp.where(above | on, both, both.T)
        pivots = diag_ref[core, tail + i // 2 : tail + i // 2 + 1, :]
        return jnp.where(on, pivots, jnp.where(above, both.T, both))

    for k in range(n):
        here = at(k)
        source = gram(k, k) if k == 0 else a_ref[here, here]
        rows = [source[at(h, SUB), :] for h in range(NB // SUB)]

        def put_upper(g, v):
            a_ref[k * NB + SUB * g : k * NB + SUB * (g + 1), here] = v

        def put_inverse(g, v):
            inv_ref[at(g, SUB), :] = v

        factor_block(rows, put_upper, put_inverse)
        if k:
            a_ref[here, : k * NB] = jnp.zeros((NB, k * NB), F32)
        inverse = inv_ref[...]
        inverse_left = left_parts(inverse)
        solved = product(left_parts(e_ref[:, here]), right_parts(inverse.T))
        if k + 1 < n:
            rest = slice((k + 1) * NB, n * NB)
            uppers, lowers, rights = {}, {}, {}
            for j in range(k + 1, n):
                uppers[j] = product(inverse_left, right_parts(gram(k, j) if k == 0 else a_ref[here, at(j)]))
                lowers[j] = left_parts(uppers[j].T)
                rights[j] = right_parts(uppers[j])
                a_ref[here, at(j)] = uppers[j]
            for i in range(k + 1, n):
                right = jnp.concatenate([rights[j] for j in range(i, n)], axis=1)
                update = product(lowers[i], right)
                for j in range(i, n):
                    old = gram(i, j) if k == 0 else a_ref[at(i), at(j)]
                    a_ref[at(i), at(j)] = old - update[:, at(j - i)]
            e_ref[:, rest] -= product(left_parts(solved), jnp.concatenate([rights[j] for j in range(k + 1, n)], axis=1))
        e_ref[:, here] = solved * scale
        tri_ref[here, :] = a_ref[here, pl.ds(pl.multiple_of(t * width, NB), width)] * (1.0 / scale)

    basis_ref[...] = e_ref[:, pl.ds(pl.multiple_of(t * width, NB), width)]


def shards(n_rows, effects):
    rows, width = effects.shape
    cols = 2 * width
    half = width // NB
    t = lax.axis_index("tensor")
    me = lax.axis_index("rows")
    swap = [(0, 1), (1, 0)]

    steps = n_rows.bit_length() - 1
    straight = [1 << j for j in range(steps)]
    crossed = straight[1::-1] + straight[2:]

    def bit(masks, j, core):
        return jnp.where(core == 0, (me // masks[0][j]) % 2, (me // masks[1][j]) % 2)

    def exchange(x, masks, j):
        perm = [(2 * r + c, 2 * (r ^ masks[c][j]) + c) for r in range(n_rows) for c in range(2)]
        return lax.ppermute(x, ("rows", "tensor"), perm)

    def sum_rows(keep, send, masks):
        got = exchange(send, masks, 0)
        yield
        total = keep + got
        for j in range(1, steps):
            piece = total.shape[0] // 2
            v = bit(masks, j, t)
            if j < steps - 1:
                sent, total = (lax.dynamic_slice_in_dim(total, i * piece, piece) for i in (1 - v, v))
                got = exchange(sent, masks, j)
            else:
                got = exchange(total, masks, j)
            yield
            total = total + got
        for j in range(steps - 2, 0, -1):
            got = exchange(total, masks, j)
            yield
            v = bit(masks, j, t)
            total = jnp.concatenate([jnp.where(v == 0, total, got), jnp.where(v == 0, got, total)])
        got = exchange(total, masks, 0)
        yield
        yield total, got, lax.ppermute(total, "tensor", swap), lax.ppermute(got, "tensor", swap)

    vmem = pl.BlockSpec(memory_space=pltpu.VMEM)
    smem = pl.BlockSpec(memory_space=pltpu.SMEM)
    params = pltpu.CompilerParams(vmem_limit_bytes=48 * 2**20)
    diag_masks, cross_masks = (straight, crossed), (crossed, straight)
    scalars = jnp.stack([t] + [bit(m, 0, core) for m in (diag_masks, cross_masks) for core in (t, 1 - t)]).astype(jnp.int32)

    grain = SUB * max(n_rows // 2, 2)
    diag_rows = (half // 2 + len(apart(half))) * NB
    diag_rows += -(-(half // 2) // grain) * grain
    cross_rows = half * half // 2 * NB

    other = lax.ppermute(effects, "tensor", swap)
    part = jax.ShapeDtypeStruct((diag_rows // 2, NB), F32)
    diag = pl.pallas_call(
        gram_diag_kernel,
        out_shape=(part, part),
        in_specs=[smem, vmem],
        out_specs=(vmem, vmem),
        scratch_shapes=[pltpu.VMEM((diag_rows, NB), F32)],
        cost_estimate=pl.CostEstimate(flops=12 * rows * diag_rows * NB, bytes_accessed=4 * rows * width, transcendentals=0),
        compiler_params=params,
        name="gram_diag",
    )(scalars, effects)
    part = jax.ShapeDtypeStruct((cross_rows // 2, NB), F32)
    cross = pl.pallas_call(
        gram_cross_kernel,
        out_shape=(part, part),
        in_specs=[smem, vmem, vmem],
        out_specs=(vmem, vmem),
        scratch_shapes=[pltpu.VMEM((rows, width), F32), pltpu.VMEM((rows, width // 2), F32), pltpu.VMEM((cross_rows, NB), F32)],
        cost_estimate=pl.CostEstimate(flops=12 * rows * cross_rows * NB, bytes_accessed=8 * rows * width, transcendentals=0),
        compiler_params=params,
        name="gram_cross",
    )(scalars, effects, other)

    diag_keep, *cross = lax.optimization_barrier((diag[0], *cross))
    diag = (diag_keep, diag[1])
    sums = []
    for pair in zip(sum_rows(*diag, diag_masks), sum_rows(*cross, cross_masks)):
        sums = pair
    scale = float(rows * n_rows) ** 0.5
    return pl.pallas_call(
        functools.partial(solve_kernel, scale),
        out_shape=(jax.ShapeDtypeStruct((rows, width), F32), jax.ShapeDtypeStruct((cols, width), F32)),
        in_specs=[smem] + [vmem] * 10,
        out_specs=(vmem, vmem),
        scratch_shapes=[
            pltpu.VMEM((2, diag_rows, NB), F32),
            pltpu.VMEM((2, cross_rows, NB), F32),
            pltpu.VMEM((cols, cols), F32),
            pltpu.VMEM((rows, cols), F32),
            pltpu.VMEM((NB, NB), F32),
        ],
        compiler_params=params,
        name="cholesky_solve",
    )(scalars, *sums[0], *sums[1], effects, other)


def solution(mesh):
    spec = P(("groups", "rows"), "tensor")
    return jax.shard_map(
        functools.partial(shards, mesh.shape["rows"]),
        mesh=mesh,
        in_specs=(spec,),
        out_specs=(spec, P("groups", "tensor")),
        check_vma=False,
    )
```

```python
import functools

import jax
import jax.numpy as jnp
from jax import lax
from jax.experimental import pallas as pl
from jax.experimental.pallas import tpu as pltpu
from jax.sharding import PartitionSpec as P

F32 = jnp.float32
BF16 = jnp.bfloat16
NB = 128
SUB = 8


def split(x):
    high = x.astype(BF16)
    rest = x - high.astype(F32)
    mid = rest.astype(BF16)
    return high, mid, (rest - mid.astype(F32)).astype(BF16)


def left_parts(x):
    h, m, l = split(x)
    return jnp.concatenate([h, h, m, m, h, l], axis=1)


def right_parts(x):
    h, m, l = split(x)
    return jnp.concatenate([h, m, h, m, l, h], axis=0)


def product(left, right):
    return jnp.dot(left, right, preferred_element_type=F32)


def row_of(x, k):
    return jnp.broadcast_to(x[k : k + 1, :], x.shape)


def lane_of(x, j):
    return jnp.broadcast_to(x[:, j : j + 1], x.shape)


def total_of(terms):
    terms = list(terms)
    while len(terms) > 1:
        terms = [terms[i] + terms[i + 1] if i + 1 < len(terms) else terms[i] for i in range(0, len(terms), 2)]
    return terms[0]


def eliminate(cols, below, parts, mine):
    zero = jnp.zeros_like(cols[0])
    pivots = zero
    taken = [x[0] for x in parts]
    for k in range(0, SUB, 2):
        a, b, e = row_of(cols[k], k), row_of(cols[k], k + 1), row_of(cols[k + 1], k + 1)
        det = a * e - b * b
        recip = 1.0 / a
        second = a * (1.0 / det)
        ratio = b * recip
        first_of = [jnp.where(mine[k], zero, cols[k]) * recip]
        last = jnp.where(mine[k], b, jnp.where(mine[k + 1], zero, cols[k + 1] - cols[k] * ratio))
        second_of = [last * second]
        if below is not None:
            reduced = below[k + 1] - below[k] * ratio
            first_of.append(below[k] * recip)
            second_of.append(reduced * second)
        pivots = jnp.where(mine[k], a, jnp.where(mine[k + 1], e - b * ratio, pivots))
        for m in range(k + 2, SUB):
            u = row_of(cols[m], k)
            w = row_of(cols[m], k + 1) - ratio * u
            cols[m] = cols[m] - first_of[0] * u - second_of[0] * w
            if below is not None:
                below[m] = below[m] - first_of[1] * u - second_of[1] * w
        if below is not None:
            for m in range(SUB):
                change = first_of[1] * row_of(below[k], m) + second_of[1] * row_of(reduced, m)
                below[SUB + m] = below[SUB + m] - change
        for i, x in enumerate(parts):
            u = row_of(x[0], k)
            w = row_of(x[0], k + 1) - ratio * u
            taken[i] = jnp.where(mine[k], x[0], jnp.where(mine[k + 1], w, taken[i]))
            for v in range(len(x)):
                x[v] = x[v] - first_of[v] * u - second_of[v] * w
    return pivots, taken


def factor_block(rows, put_upper, put_inverse):
    lane = lax.broadcasted_iota(jnp.int32, (SUB, NB), 1)
    sub = lax.broadcasted_iota(jnp.int32, (SUB, NB), 0)
    mine = [sub == k for k in range(SUB)]
    zero = jnp.zeros((SUB, NB), F32)
    rows = list(rows)
    count = len(rows)

    def emit(g, pivots, upper, inverse):
        root = lax.rsqrt(pivots)
        put_upper(g, jnp.where(lane >= sub + SUB * g, upper * root, zero))
        put_inverse(g, jnp.where(lane <= sub + SUB * g, inverse * root, zero))

    for g in range(0, count, 2):
        b = SUB * g
        col0 = [lane_of(rows[g], b + k) for k in range(SUB)]
        col1 = [lane_of(rows[g + 1], b + k) for k in range(2 * SUB)]
        near = range(g + 2, min(count, g + 4))
        factors = {h: [lane_of(rows[h], b + k) for k in range(2 * SUB)] for h in near}
        group = (lane >= b) & (lane < b + 2 * SUB)
        a = [rows[g], rows[g + 1]]
        w = [
            jnp.where(group, jnp.where(lane - b == sub, F32(1), zero), a[0]),
            jnp.where(group, jnp.where(lane - b - SUB == sub, F32(1), zero), a[1]),
        ]
        pivots, taken = eliminate(col0, col1, [a, w], mine)
        emit(g, pivots, *taken)
        recips = 1.0 / pivots
        a0, w0 = a[0] * recips, w[0] * recips
        above = [lane_of(a0, b + SUB + k) for k in range(SUB)]
        a, w = [a[1]], [w[1]]
        pivots, taken = eliminate(col1[SUB:], None, [a, w], mine)
        emit(g + 1, pivots, *taken)

        left = lane < b + 2 * SUB
        solved1 = jnp.where(left, w[0], a[0]) * (1.0 / pivots)
        lower_rows = [row_of(solved1, k) for k in range(SUB)]
        solved0 = jnp.where(left, w0, a0) - total_of(c * r for c, r in zip(above, lower_rows))
        solved = [row_of(solved0, k) for k in range(SUB)] + lower_rows
        rows[g], rows[g + 1] = solved0, solved1
        for h in near:
            rows[h] = jnp.where(group, zero, rows[h]) - total_of(f * s for f, s in zip(factors[h], solved))
        far = g + 4
        if far < count:
            panel = jnp.concatenate([rows[h] if g <= h < g + 2 else zero for h in range(count)], axis=0)
            rest = jnp.concatenate(rows[far:], axis=0)
            lanes = lax.broadcasted_iota(jnp.int32, rest.shape, 1)
            in_group = (lanes >= b) & (lanes < b + 2 * SUB)
            rest = jnp.where(in_group, F32(0), rest) - product(left_parts(rest), right_parts(panel))
            for i in range(far, count):
                rows[i] = rest[SUB * (i - far) : SUB * (i - far + 1), :]


def at(i, size=NB):
    return slice(i * size, (i + 1) * size)


def apart(n):
    return [(i, j) for i in range(n) for j in range(i + 1, n)]


def triangle_masks():
    r = lax.broadcasted_iota(jnp.int32, (NB, NB), 0)
    c = lax.broadcasted_iota(jnp.int32, (NB, NB), 1)
    return r < c, r == c


def halves(bit, all_ref, keep_ref, send_ref):
    size = keep_ref.shape[0]
    keep_ref[...] = all_ref[pl.ds(pl.multiple_of(bit * size, SUB), size), :]
    send_ref[...] = all_ref[pl.ds(pl.multiple_of((1 - bit) * size, SUB), size), :]


def square_layout(n):
    packs, offs = n // 4, len(apart(n)) // 2
    place = {(i, i): ((i // 2) // packs, (i // 2) % packs) for i in range(n)}
    place.update({ij: (number // offs, packs + number % offs) for number, ij in enumerate(apart(n))})
    return place, packs + offs


def square_products(core, start, left_of, right, out_ref):
    n = right.shape[1] // NB
    place, tail = square_layout(n)
    above, on = triangle_masks()
    for i in range(n):
        mine = [j for j in range(i, n) if place[i, j][0] == core]
        if not mine:
            continue
        row = product(left_of(i), right[:, mine[0] * NB :])
        for j in mine:
            block = row[:, at(j - mine[0])]
            where = slice(start + place[i, j][1] * NB, start + (place[i, j][1] + 1) * NB)
            if i != j:
                out_ref[where, :] = block
            elif i % 2 == 0:
                even = block
            else:
                out_ref[where, :] = jnp.where(above | on, even, block)
                pivots = jnp.sum(jnp.where(on, block, F32(0)), axis=0, keepdims=True)
                row_at = start + tail * NB + place[i, j][1]
                out_ref[row_at : row_at + 1, :] = pivots


def square_blocks(ref, start, n):
    above, on = triangle_masks()
    place, tail = square_layout(n)

    def block(i, j):
        core, number = place[i, j]
        both = ref[core, start + number * NB : start + (number + 1) * NB, :]
        if i != j:
            return both
        if i % 2 == 0:
            return jnp.where(above | on, both, both.T)
        row_at = start + tail * NB + number
        return jnp.where(on, ref[core, row_at : row_at + 1, :], jnp.where(above, both.T, both))

    return block


def copy_kernel(x_ref, out_ref):
    out_ref[...] = x_ref[...]


def gram_first_kernel(s_ref, own_ref, other_ref, keep_ref, send_ref, all_ref):
    all_ref[...] = jnp.zeros_like(all_ref)
    for core, e_ref in ((0, own_ref), (1, other_ref)):

        @pl.when(s_ref[0] == core)
        def _():
            square_products(core, 0, lambda i: left_parts(e_ref[:, at(i)].T), right_parts(e_ref[...]), all_ref)

    halves(s_ref[1], all_ref, keep_ref, send_ref)


def gram_second_kernel(s_ref, own_ref, other_ref, keep_ref, send_ref, all_ref):
    width = own_ref.shape[1]
    half = width // 2
    per_row = half // NB
    behind = width // NB * per_row * NB
    all_ref[behind:, :] = jnp.zeros((all_ref.shape[0] - behind, NB), F32)
    for core, first_ref, second_ref in ((0, own_ref, other_ref), (1, other_ref, own_ref)):

        @pl.when(s_ref[0] == core)
        def _():
            right = right_parts(second_ref[...])
            for i in range(width // NB):
                row = product(left_parts(first_ref[:, at(i)].T), right[:, core * half : (core + 1) * half])
                for j in range(per_row):
                    all_ref[at(i * per_row + j), :] = row[:, at(j)]
            square_products(core, behind, lambda i: left_parts(second_ref[:, at(i)].T), right, all_ref)

    halves(s_ref[3], all_ref, keep_ref, send_ref)


def gather_halves(t, s_ref, bit, parts, out_ref):
    size = parts[0].shape[0]
    places = ((t, s_ref[bit]), (t, 1 - s_ref[bit]), (1 - t, s_ref[bit + 1]), (1 - t, 1 - s_ref[bit + 1]))
    for (core, which), ref in zip(places, parts):
        out_ref[core, pl.ds(pl.multiple_of(which * size, SUB), size), :] = ref[...]


def factor_step(k, n, read, upper_ref, inv_ref, write):
    source = read(k, k)

    def put_upper(g, v):
        upper_ref[at(g, SUB), at(k)] = v

    def put_inverse(g, v):
        inv_ref[at(g, SUB), :] = v

    factor_block([source[at(h, SUB), :] for h in range(NB // SUB)], put_upper, put_inverse)
    if k:
        upper_ref[:, : k * NB] = jnp.zeros((NB, k * NB), F32)
    inverse = inv_ref[...]
    lowers, rights = {}, {}
    if k + 1 < n:
        inverse_left = left_parts(inverse)
        for j in range(k + 1, n):
            upper = product(inverse_left, right_parts(read(k, j)))
            lowers[j] = left_parts(upper.T)
            rights[j] = right_parts(upper)
            upper_ref[:, at(j)] = upper
        for i in range(k + 1, n):
            update = product(lowers[i], jnp.concatenate([rights[j] for j in range(i, n)], axis=1))
            for j in range(i, n):
                write(i, j, read(i, j) - update[:, at(j - i)])
    return inverse, lowers, rights


def invert_step(k, n, inverse, lowers, read, write, out_ref):
    left = left_parts(inverse)
    row = [product(left, right_parts(read(k, j))) for j in range(k)] + [inverse]
    for j, block in enumerate(row):
        out_ref[:, at(j)] = block
    if k + 1 < n:
        out_ref[:, (k + 1) * NB :] = jnp.zeros((NB, (n - k - 1) * NB), F32)
        right = right_parts(jnp.concatenate(row, axis=1))
        for i in range(k + 1, n):
            update = product(lowers[i], right)
            for j in range(k + 1):
                write(i, j, (read(i, j) if j < k else F32(0)) - update[:, at(j)])


def solve_columns(first, own_ref, other_ref, row_refs, out_refs, start):
    for k, row_ref, out_ref in zip(range(start, start + len(row_refs)), row_refs, out_refs):
        depth = (k + 1) * NB
        effects = jnp.where(first, own_ref[:, :depth], other_ref[:, :depth])
        out_ref[...] = product(left_parts(effects), right_parts(row_ref[:, :depth].T))


def start_kernel(ks, s_ref, p0, p1, p2, p3, *refs):
    sums_ref = refs[-1]
    n = refs[0].shape[1] // NB
    gather_halves(s_ref[0], s_ref, 1, (p0, p1, p2, p3), sums_ref)
    row_steps(ks, n, square_blocks(sums_ref, 0, n), None, *refs[:-1])


def next_kernel(ks, before, s_ref, own_ref, other_ref, *refs):
    row_refs, (rest_in, inv_rest_in), refs = refs[: len(before)], refs[len(before) : len(before) + 2], refs[len(before) + 2 :]
    n = own_ref.shape[1] // NB
    solve_columns(s_ref[0] == 0, own_ref, other_ref, row_refs, refs[: len(before)], before[0])

    def gram(i, j):
        return rest_in[at(i), at(j)]

    def inv_gram(i, j):
        return inv_rest_in[at(i), at(j)]

    row_steps(ks, n, gram, inv_gram, *refs[len(before) :])


def row_steps(ks, n, gram, inv_gram, *refs):
    rest_ref, inv_rest_ref, inv_ref = refs[3 * len(ks) :]

    def rest(i, j):
        return rest_ref[at(i), at(j)]

    def inv_rest(i, j):
        return inv_rest_ref[at(i), at(j)]

    for number, k in enumerate(ks):
        sources = (gram, inv_gram) if number == 0 else (rest, inv_rest)
        one_step(k, n, *sources, *refs[number : 3 * len(ks) : len(ks)], rest_ref, inv_rest_ref, inv_ref)


def one_step(k, n, gram, inv_gram, upper_ref, left_ref, row_ref, rest_ref, inv_rest_ref, inv_ref):
    def write(i, j, v):
        rest_ref[at(i), at(j)] = v

    def inv_write(i, j, v):
        inv_rest_ref[at(i), at(j)] = v

    inverse, lowers, _ = factor_step(k, n, gram, upper_ref, inv_ref, write)
    invert_step(k, n, inverse, lowers, inv_gram, inv_write, row_ref)
    left_ref[...] = left_parts(row_ref[:, : (k + 1) * NB])


def last_kernel(scale, s_ref, *refs):
    parts, (own_ref, other_ref), refs = refs[:4], refs[4:6], refs[6:]
    width = own_ref.shape[1]
    n = width // NB
    upper_refs, left_refs, first_refs, refs = refs[:n], refs[n : 2 * n], refs[2 * n : 3 * n - 1], refs[3 * n - 1 :]
    inv_row_ref, basis_ref, tri_ref, sums_ref, cross_upper_ref, work_ref, row_ref, e_ref, inv_ref, column_ref = refs
    t = s_ref[0]
    gather_halves(t, s_ref, 3, parts, sums_ref)
    gram = square_blocks(sums_ref, n * (n // 2) * NB, n)
    inverse_lefts = [ref[...] for ref in left_refs]
    lowers, rights = [], []
    for j in range(n):
        core, col = divmod(j, n // 2)
        parts = split(jnp.concatenate([sums_ref[core, at(i * (n // 2) + col), :] for i in range(n)], axis=0))
        column = []
        for k in range(n):
            h, m, l = (x[: (k + 1) * NB, :] for x in parts)
            column.append(product(inverse_lefts[k], jnp.concatenate([h, m, h, m, l, h], axis=0)))
            cross_upper_ref[at(k), at(j)] = column[k]
        column = jnp.concatenate(column, axis=0)
        lowers.append(left_parts(column.T))
        rights.append(right_parts(column))
    for i in range(n):
        update = product(lowers[i], jnp.concatenate(rights[i:], axis=1))
        for j in range(i, n):
            work_ref[at(i), at(j)] = gram(i, j) - update[:, at(j - i)]
    solve_columns(t == 0, own_ref, other_ref, [inv_row_ref], [column_ref], n - 1)
    first_refs = (*first_refs, column_ref)
    solved = jnp.concatenate([ref[...] for ref in first_refs], axis=1)
    effects = jnp.where(t == 0, other_ref[...], own_ref[...])
    e_ref[...] = effects - product(left_parts(solved), jnp.concatenate(rights, axis=1))

    def read(i, j):
        return work_ref[at(i), at(j)]

    def write(i, j, v):
        work_ref[at(i), at(j)] = v

    first = t == 0
    for k in range(n):
        tri_ref[at(k), :] = jnp.where(first, upper_refs[k][...], cross_upper_ref[at(k), :]) * (1.0 / scale)
    for k in range(n):
        inverse, _, rights = factor_step(k, n, read, row_ref, inv_ref, write)
        solved = product(left_parts(e_ref[:, at(k)]), right_parts(inverse.T))
        if k + 1 < n:
            later = jnp.concatenate([rights[j] for j in range(k + 1, n)], axis=1)
            e_ref[:, (k + 1) * NB :] -= product(left_parts(solved), later)
        basis_ref[:, at(k)] = jnp.where(first, first_refs[k][...], solved) * scale
        tri_ref[at(n + k), :] = jnp.where(first, F32(0), row_ref[...] * (1.0 / scale))


def shards(n_rows, effects):
    rows, width = effects.shape
    cols = 2 * width
    half = width // NB
    t = lax.axis_index("tensor")
    me = lax.axis_index("rows")
    swap = [(0, 1), (1, 0)]

    steps = n_rows.bit_length() - 1
    straight = [1 << j for j in range(steps)]
    crossed = straight[1::-1] + straight[2:]

    def bit(masks, j, core):
        return jnp.where(core == 0, (me // masks[0][j]) % 2, (me // masks[1][j]) % 2)

    def exchange(x, masks, j):
        perm = [(2 * r + c, 2 * (r ^ masks[c][j]) + c) for r in range(n_rows) for c in range(2)]
        return lax.ppermute(x, ("rows", "tensor"), perm)

    def sum_rows(keep, send, masks):
        def tie(got, gate):
            return got if gate is None else lax.optimization_barrier((got, gate))[0]

        got = exchange(send, masks, 0)
        total = keep + tie(got, (yield keep))
        for j in range(1, steps - 1):
            piece = total.shape[0] // 2
            v = bit(masks, j, t)
            sent, total = (lax.dynamic_slice_in_dim(total, i * piece, piece) for i in (1 - v, v))
            got = exchange(sent, masks, j)
            total = total + tie(got, (yield total))
        got = exchange(total, masks, steps - 1)
        total = total + tie(got, (yield total))
        for j in range(steps - 2, 0, -1):
            got = exchange(total, masks, j)
            got = tie(got, (yield total))
            v = bit(masks, j, t)
            total = jnp.concatenate([jnp.where(v == 0, total, got), jnp.where(v == 0, got, total)])
        got = exchange(total, masks, 0)
        got = tie(got, (yield total))
        yield total, got, lax.ppermute(total, "tensor", swap), lax.ppermute(got, "tensor", swap)

    vmem = pl.BlockSpec(memory_space=pltpu.VMEM)
    smem = pl.BlockSpec(memory_space=pltpu.SMEM)
    params = pltpu.CompilerParams(vmem_limit_bytes=20 * 2**20)

    def array(*shape):
        return jax.ShapeDtypeStruct(shape, F32)

    def call(kernel, name, out_shape, scratch, *args):
        scalar = [a.dtype == jnp.int32 for a in args]
        return pl.pallas_call(
            kernel,
            out_shape=out_shape,
            in_specs=[smem if s else vmem for s in scalar],
            out_specs=tuple(vmem for _ in out_shape),
            scratch_shapes=[pltpu.VMEM(shape, F32) for shape in scratch],
            cost_estimate=pl.CostEstimate(flops=0, bytes_accessed=0, transcendentals=0),
            compiler_params=params,
            name=name,
        )(*args)

    first_masks, second_masks = (straight, crossed), (crossed, straight)
    scalars = jnp.stack([t] + [bit(m, 0, core) for m in (first_masks, second_masks) for core in (t, 1 - t)]).astype(jnp.int32)

    grain = SUB * max(n_rows // 2, 2)
    first_rows = square_layout(half)[1] * NB
    second_rows = first_rows + half * half // 2 * NB
    first_rows, second_rows = (x + -(-(half // 4) // grain) * grain for x in (first_rows, second_rows))

    other = lax.ppermute(effects, "tensor", swap)
    def halves_of(size):
        return (array(size // 2, NB),) * 2

    (own,) = call(copy_kernel, "own_copy", (array(rows, width),), [], effects)
    first = call(gram_first_kernel, "gram_first", halves_of(first_rows), [(first_rows, NB)], scalars, own, other)
    second = call(gram_second_kernel, "gram_second", halves_of(second_rows), [(second_rows, NB)], scalars, own, other)
    first_keep, *second = lax.optimization_barrier((first[0], *second))
    one, two = sum_rows(first_keep, first[1], first_masks), sum_rows(*second, second_masks)
    next(one), next(two)
    stages = 2 * steps - 1
    for i in range(stages):
        first_sums = one.send(None)
        if i >= 2:
            two.send(None)

    uppers, lefts, inverse_rows, solved = [], [], [], []
    rest = first_sums
    before = []
    for ks in ([0], list(range(1, half - 1)), [half - 1]):
        columns = [array(rows, NB) for _ in before]
        out = [array(NB, width) for _ in ks]
        out += [jax.ShapeDtypeStruct((NB, 6 * (k + 1) * NB), BF16) for k in ks]
        out += [array(NB, width) for _ in ks] + [array(width, width), array(width, width)]
        if before:
            kernel, scratch = functools.partial(next_kernel, ks, before), [(NB, NB)]
            args = (scalars, own, other, *inverse_rows[before[0] :], *rest)
        else:
            kernel, scratch = functools.partial(start_kernel, ks), [(NB, NB), (2, first_rows, NB)]
            args = (scalars, *rest)
        *made, rest_rows, rest_inverse = call(kernel, "factor_rows", columns + out, scratch, *args)
        rest = (rest_rows, rest_inverse)
        solved += made[: len(before)]
        made = made[len(before) :]
        for group, number in ((uppers, 0), (lefts, 1), (inverse_rows, 2)):
            group += made[number * len(ks) : (number + 1) * len(ks)]
        before = ks

    for gate in (uppers[0], uppers[-2]):
        second_sums = two.send(gate)
    scale = float(rows * n_rows) ** 0.5
    scratch = [(2, second_rows, NB), (width, width), (width, width), (NB, width), (rows, width), (NB, NB), (rows, NB)]
    return call(
        functools.partial(last_kernel, scale),
        "factor_last",
        (array(rows, width), array(cols, width)),
        scratch,
        *(scalars, *second_sums, own, other, *uppers, *lefts, *solved, *inverse_rows[before[0] :]),
    )


def solution(mesh):
    spec = P(("groups", "rows"), "tensor")
    return jax.shard_map(
        functools.partial(shards, mesh.shape["rows"]),
        mesh=mesh,
        in_specs=(spec,),
        out_specs=(spec, P("groups", "tensor")),
        check_vma=False,
    )
```

```python
import functools

import jax
import jax.numpy as jnp
from jax import lax
from jax.experimental import pallas as pl
from jax.experimental.pallas import tpu as pltpu
from jax.sharding import PartitionSpec as P

F32 = jnp.float32
BF16 = jnp.bfloat16
NB = 128
SUB = 8


def split(x):
    high = x.astype(BF16)
    rest = x - high.astype(F32)
    mid = rest.astype(BF16)
    return high, mid, (rest - mid.astype(F32)).astype(BF16)


def left_parts(x):
    h, m, l = split(x)
    return jnp.concatenate([h, h, m, m, h, l], axis=1)


def right_parts(x):
    h, m, l = split(x)
    return jnp.concatenate([h, m, h, m, l, h], axis=0)


def product(left, right):
    return jnp.dot(left, right, preferred_element_type=F32)


def column_parts(x):
    h, m, l = split(x)
    return jnp.concatenate([h, h, m, m, h, l], axis=0), jnp.concatenate([h, m, h, m, l, h], axis=0)


def product_of_columns(left, right):
    return lax.dot_general(left, right, (((0,), (0,)), ((), ())), preferred_element_type=F32)


def row_of(x, k):
    return jnp.broadcast_to(x[k : k + 1, :], x.shape)


def lane_of(x, j):
    return jnp.broadcast_to(x[:, j : j + 1], x.shape)


def total_of(terms):
    terms = list(terms)
    while len(terms) > 1:
        terms = [terms[i] + terms[i + 1] if i + 1 < len(terms) else terms[i] for i in range(0, len(terms), 2)]
    return terms[0]


def eliminate(cols, below, parts, mine):
    zero = jnp.zeros_like(cols[0])
    pivots = zero
    taken = [x[0] for x in parts]
    for k in range(0, SUB, 2):
        a, b, e = row_of(cols[k], k), row_of(cols[k], k + 1), row_of(cols[k + 1], k + 1)
        det = a * e - b * b
        recip = 1.0 / a
        second = a * (1.0 / det)
        ratio = b * recip
        first_of = [jnp.where(mine[k], zero, cols[k]) * recip]
        last = jnp.where(mine[k], b, jnp.where(mine[k + 1], zero, cols[k + 1] - cols[k] * ratio))
        second_of = [last * second]
        if below is not None:
            reduced = below[k + 1] - below[k] * ratio
            first_of.append(below[k] * recip)
            second_of.append(reduced * second)
        pivots = jnp.where(mine[k], a, jnp.where(mine[k + 1], e - b * ratio, pivots))
        for m in range(k + 2, SUB):
            u = row_of(cols[m], k)
            w = row_of(cols[m], k + 1) - ratio * u
            cols[m] = cols[m] - first_of[0] * u - second_of[0] * w
            if below is not None:
                below[m] = below[m] - first_of[1] * u - second_of[1] * w
        if below is not None:
            for m in range(SUB):
                change = first_of[1] * row_of(below[k], m) + second_of[1] * row_of(reduced, m)
                below[SUB + m] = below[SUB + m] - change
        for i, x in enumerate(parts):
            u = row_of(x[0], k)
            w = row_of(x[0], k + 1) - ratio * u
            taken[i] = jnp.where(mine[k], x[0], jnp.where(mine[k + 1], w, taken[i]))
            for v in range(len(x)):
                x[v] = x[v] - first_of[v] * u - second_of[v] * w
    return pivots, taken


def run_share(pending, turns):
    for _ in range(-(-len(pending) // turns)):
        pending.pop(0)()


def factor_block(rows, put_upper, put_inverse, pending):
    lane = lax.broadcasted_iota(jnp.int32, (SUB, NB), 1)
    sub = lax.broadcasted_iota(jnp.int32, (SUB, NB), 0)
    mine = [sub == k for k in range(SUB)]
    zero = jnp.zeros((SUB, NB), F32)
    rows = list(rows)
    count = len(rows)

    def emit(g, pivots, upper, inverse):
        root = lax.rsqrt(pivots)
        put_upper(g, jnp.where(lane >= sub + SUB * g, upper * root, zero))
        put_inverse(g, jnp.where(lane <= sub + SUB * g, inverse * root, zero))

    for g in range(0, count, 2):
        b = SUB * g
        col0 = [lane_of(rows[g], b + k) for k in range(SUB)]
        col1 = [lane_of(rows[g + 1], b + k) for k in range(2 * SUB)]
        near = range(g + 2, min(count, g + 4))
        factors = {h: [lane_of(rows[h], b + k) for k in range(2 * SUB)] for h in near}
        run_share(pending, (count - g) // 2)
        group = (lane >= b) & (lane < b + 2 * SUB)
        a = [rows[g], rows[g + 1]]
        w = [
            jnp.where(group, jnp.where(lane - b == sub, F32(1), zero), a[0]),
            jnp.where(group, jnp.where(lane - b - SUB == sub, F32(1), zero), a[1]),
        ]
        pivots, taken = eliminate(col0, col1, [a, w], mine)
        emit(g, pivots, *taken)
        recips = 1.0 / pivots
        a0, w0 = a[0] * recips, w[0] * recips
        above = [lane_of(a0, b + SUB + k) for k in range(SUB)]
        a, w = [a[1]], [w[1]]
        pivots, taken = eliminate(col1[SUB:], None, [a, w], mine)
        emit(g + 1, pivots, *taken)

        left = lane < b + 2 * SUB
        solved1 = jnp.where(left, w[0], a[0]) * (1.0 / pivots)
        lower_rows = [row_of(solved1, k) for k in range(SUB)]
        solved0 = jnp.where(left, w0, a0) - total_of(c * r for c, r in zip(above, lower_rows))
        solved = [row_of(solved0, k) for k in range(SUB)] + lower_rows
        rows[g], rows[g + 1] = solved0, solved1
        for h in near:
            rows[h] = jnp.where(group, zero, rows[h]) - total_of(f * s for f, s in zip(factors[h], solved))
        far = g + 4
        if far < count:
            panel = jnp.concatenate([rows[h] if g <= h < g + 2 else zero for h in range(count)], axis=0)
            rest = jnp.concatenate(rows[far:], axis=0)
            lanes = lax.broadcasted_iota(jnp.int32, rest.shape, 1)
            in_group = (lanes >= b) & (lanes < b + 2 * SUB)
            rest = jnp.where(in_group, F32(0), rest) - product(left_parts(rest), right_parts(panel))
            for i in range(far, count):
                rows[i] = rest[SUB * (i - far) : SUB * (i - far + 1), :]


def at(i, size=NB):
    return slice(i * size, (i + 1) * size)


def apart(n):
    return [(i, j) for i in range(n) for j in range(i + 1, n)]


def triangle_masks():
    r = lax.broadcasted_iota(jnp.int32, (NB, NB), 0)
    c = lax.broadcasted_iota(jnp.int32, (NB, NB), 1)
    return r < c, r == c


def halves(bit, all_ref, keep_ref, send_ref):
    size = keep_ref.shape[0]
    keep_ref[...] = all_ref[pl.ds(pl.multiple_of(bit * size, SUB), size), :]
    send_ref[...] = all_ref[pl.ds(pl.multiple_of((1 - bit) * size, SUB), size), :]


def square_layout(n):
    packs, offs = n // 4, len(apart(n)) // 2
    place = {(i, i): ((i // 2) // packs, (i // 2) % packs) for i in range(n)}
    place.update({ij: (number // offs, packs + number % offs) for number, ij in enumerate(apart(n))})
    return place, packs + offs


def square_products(core, start, left_of, right, out_ref):
    n = right.shape[1] // NB
    place, tail = square_layout(n)
    above, on = triangle_masks()
    for i in range(n):
        mine = [j for j in range(i, n) if place[i, j][0] == core]
        if not mine:
            continue
        row = product(left_of(i), right[:, mine[0] * NB :])
        for j in mine:
            block = row[:, at(j - mine[0])]
            where = slice(start + place[i, j][1] * NB, start + (place[i, j][1] + 1) * NB)
            if i != j:
                out_ref[where, :] = block
            elif i % 2 == 0:
                even = block
            else:
                out_ref[where, :] = jnp.where(above | on, even, block)
                pivots = jnp.sum(jnp.where(on, block, F32(0)), axis=0, keepdims=True)
                row_at = start + tail * NB + place[i, j][1]
                out_ref[row_at : row_at + 1, :] = pivots


def square_blocks(ref, start, n):
    above, on = triangle_masks()
    place, tail = square_layout(n)

    def block(i, j):
        core, number = place[i, j]
        both = ref[core, start + number * NB : start + (number + 1) * NB, :]
        if i != j:
            return both
        if i % 2 == 0:
            return jnp.where(above | on, both, both.T)
        row_at = start + tail * NB + number
        return jnp.where(on, ref[core, row_at : row_at + 1, :], jnp.where(above, both.T, both))

    return block


def copy_kernel(x_ref, out_ref):
    out_ref[...] = x_ref[...]


def gram_first_kernel(s_ref, own_ref, other_ref, keep_ref, send_ref, all_ref):
    all_ref[...] = jnp.zeros_like(all_ref)
    for core, e_ref in ((0, own_ref), (1, other_ref)):

        @pl.when(s_ref[0] == core)
        def _():
            square_products(core, 0, lambda i: left_parts(e_ref[:, at(i)].T), right_parts(e_ref[...]), all_ref)

    halves(s_ref[1], all_ref, keep_ref, send_ref)


def gram_second_kernel(s_ref, own_ref, other_ref, keep_ref, send_ref, all_ref):
    width = own_ref.shape[1]
    half = width // 2
    per_row = half // NB
    behind = width // NB * per_row * NB
    all_ref[behind:, :] = jnp.zeros((all_ref.shape[0] - behind, NB), F32)
    for core, first_ref, second_ref in ((0, own_ref, other_ref), (1, other_ref, own_ref)):

        @pl.when(s_ref[0] == core)
        def _():
            right = right_parts(second_ref[...])
            for i in range(width // NB):
                row = product(left_parts(first_ref[:, at(i)].T), right[:, core * half : (core + 1) * half])
                for j in range(per_row):
                    all_ref[at(i * per_row + j), :] = row[:, at(j)]
            square_products(core, behind, lambda i: left_parts(second_ref[:, at(i)].T), right, all_ref)

    halves(s_ref[3], all_ref, keep_ref, send_ref)


def gather_halves(t, s_ref, bit, parts, out_ref):
    size = parts[0].shape[0]
    places = ((t, s_ref[bit]), (t, 1 - s_ref[bit]), (1 - t, s_ref[bit + 1]), (1 - t, 1 - s_ref[bit + 1]))
    for (core, which), ref in zip(places, parts):
        out_ref[core, pl.ds(pl.multiple_of(which * size, SUB), size), :] = ref[...]


def factor_step(k, n, read, upper_ref, inv_ref, write, pending):
    source = read(k, k)

    def put_upper(g, v):
        upper_ref[at(g, SUB), at(k)] = v

    def put_inverse(g, v):
        inv_ref[at(g, SUB), :] = v

    factor_block([source[at(h, SUB), :] for h in range(NB // SUB)], put_upper, put_inverse, pending)
    if k:
        upper_ref[:, : k * NB] = jnp.zeros((NB, k * NB), F32)
    inverse = inv_ref[...]
    lowers, rights = {}, {}
    if k + 1 < n:
        inverse_left = left_parts(inverse)

        def upper_block(j):
            upper = product(inverse_left, right_parts(read(k, j)))
            lowers[j], rights[j] = column_parts(upper)
            upper_ref[:, at(j)] = upper

        def update(i, columns):
            change = product_of_columns(lowers[i], jnp.concatenate([rights[j] for j in columns], axis=1))
            for number, j in enumerate(columns):
                write(i, j, read(i, j) - change[:, at(number)])

        upper_block(k + 1)
        update(k + 1, [k + 1])
        pending += [functools.partial(upper_block, j) for j in range(k + 2, n)]
        if k + 2 < n:
            pending.append(functools.partial(update, k + 1, range(k + 2, n)))
        pending += [functools.partial(update, i, range(i, n)) for i in range(k + 2, n)]
    return inverse, lowers, rights


def invert_step(k, n, inverse, lowers, read, write, out_ref, left_ref, pending):
    right = []

    def own_row():
        left = left_parts(inverse)
        row = [product(left, right_parts(read(k, j))) for j in range(k)] + [inverse]
        for j, block in enumerate(row):
            out_ref[:, at(j)] = block
        if k + 1 < n:
            out_ref[:, (k + 1) * NB :] = jnp.zeros((NB, (n - k - 1) * NB), F32)
        row = jnp.concatenate(row, axis=1)
        right.append(right_parts(row))
        left_ref[...] = left_parts(row)

    def update(i):
        change = product_of_columns(lowers[i], right[0])
        for j in range(k + 1):
            write(i, j, (read(i, j) if j < k else F32(0)) - change[:, at(j)])

    pending.append(own_row)
    pending += [functools.partial(update, i) for i in range(k + 1, n)]


def solve_columns(first, own_ref, other_ref, row_refs, out_refs, start):
    def column(k, row_ref, out_ref):
        depth = (k + 1) * NB
        effects = jnp.where(first, own_ref[:, :depth], other_ref[:, :depth])
        out_ref[...] = product(left_parts(effects), right_parts(row_ref[:, :depth].T))

    return [functools.partial(column, k, *refs) for k, *refs in zip(range(start, start + len(row_refs)), row_refs, out_refs)]


def start_kernel(ks, s_ref, p0, p1, p2, p3, *refs):
    sums_ref = refs[-1]
    n = refs[0].shape[1] // NB
    gather_halves(s_ref[0], s_ref, 1, (p0, p1, p2, p3), sums_ref)
    row_steps(ks, n, square_blocks(sums_ref, 0, n), None, [], *refs[:-1])


def next_kernel(ks, before, s_ref, own_ref, other_ref, *refs):
    row_refs, (rest_in, inv_rest_in), refs = refs[: len(before)], refs[len(before) : len(before) + 2], refs[len(before) + 2 :]
    n = own_ref.shape[1] // NB
    pending = solve_columns(s_ref[0] == 0, own_ref, other_ref, row_refs, refs[: len(before)], before[0])

    def gram(i, j):
        return rest_in[at(i), at(j)]

    def inv_gram(i, j):
        return inv_rest_in[at(i), at(j)]

    row_steps(ks, n, gram, inv_gram, pending, *refs[len(before) :])


def row_steps(ks, n, gram, inv_gram, pending, *refs):
    rest_ref, inv_rest_ref, inv_ref = refs[3 * len(ks) :]

    def rest(i, j):
        return rest_ref[at(i), at(j)]

    def inv_rest(i, j):
        return inv_rest_ref[at(i), at(j)]

    for number, k in enumerate(ks):
        sources = (gram, inv_gram) if number == 0 else (rest, inv_rest)
        one_step(k, n, *sources, pending, *refs[number : 3 * len(ks) : len(ks)], rest_ref, inv_rest_ref, inv_ref)
    run_share(pending, 1)


def one_step(k, n, gram, inv_gram, pending, upper_ref, left_ref, row_ref, rest_ref, inv_rest_ref, inv_ref):
    def write(i, j, v):
        rest_ref[at(i), at(j)] = v

    def inv_write(i, j, v):
        inv_rest_ref[at(i), at(j)] = v

    inverse, lowers, _ = factor_step(k, n, gram, upper_ref, inv_ref, write, pending)
    invert_step(k, n, inverse, lowers, inv_gram, inv_write, row_ref, left_ref, pending)


def last_kernel(scale, s_ref, *refs):
    parts, (own_ref, other_ref), refs = refs[:4], refs[4:6], refs[6:]
    width = own_ref.shape[1]
    n = width // NB
    upper_refs, left_refs, first_refs, refs = refs[:n], refs[n : 2 * n], refs[2 * n : 3 * n - 1], refs[3 * n - 1 :]
    inv_row_ref, basis_ref, tri_ref, sums_ref, cross_upper_ref, work_ref, row_ref, e_ref, inv_ref, column_ref = refs
    t = s_ref[0]
    gather_halves(t, s_ref, 3, parts, sums_ref)
    gram = square_blocks(sums_ref, n * (n // 2) * NB, n)
    first = t == 0
    lowers, rights = {}, {}

    def cross_column(j):
        core, col = divmod(j, n // 2)
        parts = split(jnp.concatenate([sums_ref[core, at(i * (n // 2) + col), :] for i in range(n)], axis=0))
        column = []
        for k in range(n):
            h, m, l = (x[: (k + 1) * NB, :] for x in parts)
            column.append(product(left_refs[k][...], jnp.concatenate([h, m, h, m, l, h], axis=0)))
            cross_upper_ref[at(k), at(j)] = column[k]
        column = jnp.concatenate(column, axis=0)
        lowers[j], rights[j] = column_parts(column)

    def take_off(i, columns):
        change = product_of_columns(lowers[i], jnp.concatenate([rights[j] for j in columns], axis=1))
        for number, j in enumerate(columns):
            work_ref[at(i), at(j)] = gram(i, j) - change[:, at(number)]

    def take_off_effects():
        solved = jnp.concatenate([ref[...] for ref in (*first_refs, column_ref)], axis=1)
        effects = jnp.where(first, other_ref[...], own_ref[...])
        e_ref[...] = effects - product(left_parts(solved), jnp.concatenate([rights[j] for j in range(n)], axis=1))

    def upper_rows(k):
        tri_ref[at(k), :] = jnp.where(first, upper_refs[k][...], cross_upper_ref[at(k), :]) * (1.0 / scale)

    def solve_effects(k, inverse, rights):
        solved = product(left_parts(e_ref[:, at(k)]), right_parts(inverse.T))
        if k + 1 < n:
            later = jnp.concatenate([rights[j] for j in range(k + 1, n)], axis=1)
            e_ref[:, (k + 1) * NB :] -= product(left_parts(solved), later)
        done = first_refs[k] if k + 1 < n else column_ref
        basis_ref[:, at(k)] = jnp.where(first, done[...], solved) * scale
        tri_ref[at(n + k), :] = jnp.where(first, F32(0), row_ref[k % 2] * (1.0 / scale))

    def read(i, j):
        return work_ref[at(i), at(j)]

    def write(i, j, v):
        work_ref[at(i), at(j)] = v

    cross_column(0)
    take_off(0, [0])
    pending = [functools.partial(cross_column, j) for j in range(1, n)]
    pending.append(functools.partial(take_off, 0, range(1, n)))
    pending += [functools.partial(take_off, i, range(i, n)) for i in range(1, n)]
    pending += solve_columns(first, own_ref, other_ref, [inv_row_ref], [column_ref], n - 1)
    pending.append(take_off_effects)
    pending += [functools.partial(upper_rows, k) for k in range(n)]
    for k in range(n):
        inverse, _, row_rights = factor_step(k, n, read, row_ref.at[k % 2], inv_ref, write, pending)
        pending.append(functools.partial(solve_effects, k, inverse, row_rights))
    run_share(pending, 1)


def shards(n_rows, effects):
    rows, width = effects.shape
    cols = 2 * width
    half = width // NB
    t = lax.axis_index("tensor")
    me = lax.axis_index("rows")
    swap = [(0, 1), (1, 0)]

    steps = n_rows.bit_length() - 1
    straight = [1 << j for j in range(steps)]
    crossed = straight[1::-1] + straight[2:]

    def bit(masks, j, core):
        return jnp.where(core == 0, (me // masks[0][j]) % 2, (me // masks[1][j]) % 2)

    def exchange(x, masks, j):
        perm = [(2 * r + c, 2 * (r ^ masks[c][j]) + c) for r in range(n_rows) for c in range(2)]
        return lax.ppermute(x, ("rows", "tensor"), perm)

    def sum_rows(keep, send, masks):
        def tie(got, gate):
            return got if gate is None else lax.optimization_barrier((got, gate))[0]

        got = exchange(send, masks, 0)
        total = keep + tie(got, (yield keep))
        for j in range(1, steps - 1):
            piece = total.shape[0] // 2
            v = bit(masks, j, t)
            sent, total = (lax.dynamic_slice_in_dim(total, i * piece, piece) for i in (1 - v, v))
            got = exchange(sent, masks, j)
            total = total + tie(got, (yield total))
        got = exchange(total, masks, steps - 1)
        total = total + tie(got, (yield total))
        for j in range(steps - 2, 0, -1):
            got = exchange(total, masks, j)
            got = tie(got, (yield total))
            v = bit(masks, j, t)
            total = jnp.concatenate([jnp.where(v == 0, total, got), jnp.where(v == 0, got, total)])
        got = exchange(total, masks, 0)
        got = tie(got, (yield total))
        yield total, got, lax.ppermute(total, "tensor", swap), lax.ppermute(got, "tensor", swap)

    vmem = pl.BlockSpec(memory_space=pltpu.VMEM)
    smem = pl.BlockSpec(memory_space=pltpu.SMEM)
    params = pltpu.CompilerParams(vmem_limit_bytes=20 * 2**20)

    def array(*shape):
        return jax.ShapeDtypeStruct(shape, F32)

    def call(kernel, name, out_shape, scratch, *args):
        scalar = [a.dtype == jnp.int32 for a in args]
        return pl.pallas_call(
            kernel,
            out_shape=out_shape,
            in_specs=[smem if s else vmem for s in scalar],
            out_specs=tuple(vmem for _ in out_shape),
            scratch_shapes=[pltpu.VMEM(shape, F32) for shape in scratch],
            cost_estimate=pl.CostEstimate(flops=0, bytes_accessed=0, transcendentals=0),
            compiler_params=params,
            name=name,
        )(*args)

    first_masks, second_masks = (straight, crossed), (crossed, straight)
    scalars = jnp.stack([t] + [bit(m, 0, core) for m in (first_masks, second_masks) for core in (t, 1 - t)]).astype(jnp.int32)

    grain = SUB * max(n_rows // 2, 2)
    first_rows = square_layout(half)[1] * NB
    second_rows = first_rows + half * half // 2 * NB
    first_rows, second_rows = (x + -(-(half // 4) // grain) * grain for x in (first_rows, second_rows))

    other = lax.ppermute(effects, "tensor", swap)
    def halves_of(size):
        return (array(size // 2, NB),) * 2

    (own,) = call(copy_kernel, "own_copy", (array(rows, width),), [], effects)
    first = call(gram_first_kernel, "gram_first", halves_of(first_rows), [(first_rows, NB)], scalars, own, other)
    second = call(gram_second_kernel, "gram_second", halves_of(second_rows), [(second_rows, NB)], scalars, own, other)
    first_keep, *second = lax.optimization_barrier((first[0], *second))
    one, two = sum_rows(first_keep, first[1], first_masks), sum_rows(*second, second_masks)
    next(one), next(two)
    stages = 2 * steps - 1
    for i in range(stages):
        first_sums = one.send(None)
        if i >= 2:
            two.send(None)

    uppers, lefts, inverse_rows, solved = [], [], [], []
    rest = first_sums
    before = []
    for ks in ([0], list(range(1, half - 1)), [half - 1]):
        columns = [array(rows, NB) for _ in before]
        out = [array(NB, width) for _ in ks]
        out += [jax.ShapeDtypeStruct((NB, 6 * (k + 1) * NB), BF16) for k in ks]
        out += [array(NB, width) for _ in ks]
        final = ks[-1] == half - 1
        out += [] if final else [array(width, width), array(width, width)]
        if before:
            kernel, scratch = functools.partial(next_kernel, ks, before), ([(SUB, NB)] * 2 if final else []) + [(NB, NB)]
            args = (scalars, own, other, *inverse_rows[before[0] :], *rest)
        else:
            kernel, scratch = functools.partial(start_kernel, ks), [(NB, NB), (2, first_rows, NB)]
            args = (scalars, *rest)
        made = call(kernel, "factor_rows", columns + out, scratch, *args)
        rest = made[-2:]
        solved += made[: len(before)]
        made = made[len(before) :]
        for group, number in ((uppers, 0), (lefts, 1), (inverse_rows, 2)):
            group += made[number * len(ks) : (number + 1) * len(ks)]
        before = ks

    for gate in (uppers[0], uppers[-2]):
        second_sums = two.send(gate)
    scale = float(rows * n_rows) ** 0.5
    scratch = [(2, second_rows, NB), (width, width), (width, width), (2, NB, width), (rows, width), (NB, NB), (rows, NB)]
    return call(
        functools.partial(last_kernel, scale),
        "factor_last",
        (array(rows, width), array(cols, width)),
        scratch,
        *(scalars, *second_sums, own, other, *uppers, *lefts, *solved, *inverse_rows[before[0] :]),
    )


def solution(mesh):
    spec = P(("groups", "rows"), "tensor")
    return jax.shard_map(
        functools.partial(shards, mesh.shape["rows"]),
        mesh=mesh,
        in_specs=(spec,),
        out_specs=(spec, P("groups", "tensor")),
        check_vma=False,
    )
```

```python
import functools

import jax
import jax.numpy as jnp
from jax import lax
from jax.experimental import pallas as pl
from jax.experimental.pallas import tpu as pltpu
from jax.sharding import PartitionSpec as P

F32 = jnp.float32
BF16 = jnp.bfloat16
NB = 128
SUB = 8
ROOT_SCALE = 2.0**20


def split(x):
    high = x.astype(BF16)
    rest = x - high.astype(F32)
    mid = rest.astype(BF16)
    return high, mid, (rest - mid.astype(F32)).astype(BF16)


def left_parts(x):
    h, m, l = split(x)
    return jnp.concatenate([h, h, m, m, h, l], axis=1)


def right_parts(x):
    h, m, l = split(x)
    return jnp.concatenate([h, m, h, m, l, h], axis=0)


def product(left, right):
    return jnp.dot(left, right, preferred_element_type=F32)


def column_parts(x):
    h, m, l = split(x)
    return jnp.concatenate([h, h, m, m, h, l], axis=0), jnp.concatenate([h, m, h, m, l, h], axis=0)


def product_of_columns(left, right):
    return lax.dot_general(left, right, (((0,), (0,)), ((), ())), preferred_element_type=F32)


def row_of(x, k):
    return jnp.broadcast_to(x[k : k + 1, :], x.shape)


def lane_of(x, j):
    return jnp.broadcast_to(x[:, j : j + 1], x.shape)


def total_of(terms):
    terms = list(terms)
    while len(terms) > 1:
        terms = [terms[i] + terms[i + 1] if i + 1 < len(terms) else terms[i] for i in range(0, len(terms), 2)]
    return terms[0]


def eliminate(cols, below, parts, mine):
    zero = jnp.zeros_like(cols[0])
    pivots = zero
    taken = [x[0] for x in parts]
    for k in range(0, SUB, 2):
        a, b, e = row_of(cols[k], k), row_of(cols[k], k + 1), row_of(cols[k + 1], k + 1)
        det = a * e - b * b
        recip = 1.0 / a
        second = a * (1.0 / det)
        ratio = b * recip
        first_of = [jnp.where(mine[k], zero, cols[k]) * recip]
        last = jnp.where(mine[k], b, jnp.where(mine[k + 1], zero, cols[k + 1] - cols[k] * ratio))
        second_of = [last * second]
        if below is not None:
            reduced = below[k + 1] - below[k] * ratio
            first_of.append(below[k] * recip)
            second_of.append(reduced * second)
        pivots = jnp.where(mine[k], a, jnp.where(mine[k + 1], e - b * ratio, pivots))
        for m in range(k + 2, SUB):
            u = row_of(cols[m], k)
            w = row_of(cols[m], k + 1) - ratio * u
            cols[m] = cols[m] - first_of[0] * u - second_of[0] * w
            if below is not None:
                below[m] = below[m] - first_of[1] * u - second_of[1] * w
        if below is not None:
            for m in range(SUB):
                change = first_of[1] * row_of(below[k], m) + second_of[1] * row_of(reduced, m)
                below[SUB + m] = below[SUB + m] - change
        for i, x in enumerate(parts):
            u = row_of(x[0], k)
            w = row_of(x[0], k + 1) - ratio * u
            taken[i] = jnp.where(mine[k], x[0], jnp.where(mine[k + 1], w, taken[i]))
            for v in range(len(x)):
                x[v] = x[v] - first_of[v] * u - second_of[v] * w
    return pivots, taken


def run_share(pending, turns):
    for _ in range(-(-len(pending) // turns)):
        pending.pop(0)()


def factor_block(rows, put_upper, put_inverse, pending):
    lane = lax.broadcasted_iota(jnp.int32, (SUB, NB), 1)
    sub = lax.broadcasted_iota(jnp.int32, (SUB, NB), 0)
    mine = [sub == k for k in range(SUB)]
    zero = jnp.zeros((SUB, NB), F32)
    rows = list(rows)
    count = len(rows)

    def emit(g, pivots, upper, inverse):
        root = lax.rsqrt(pivots)
        put_upper(g, jnp.where(lane >= sub + SUB * g, upper * root, zero))
        put_inverse(g, jnp.where(lane <= sub + SUB * g, inverse * root, zero))

    for g in range(0, count, 2):
        b = SUB * g
        col0 = [lane_of(rows[g], b + k) for k in range(SUB)]
        col1 = [lane_of(rows[g + 1], b + k) for k in range(2 * SUB)]
        near = range(g + 2, min(count, g + 4))
        factors = {h: [lane_of(rows[h], b + k) for k in range(2 * SUB)] for h in near}
        run_share(pending, (count - g) // 2)
        group = (lane >= b) & (lane < b + 2 * SUB)
        a = [rows[g], rows[g + 1]]
        w = [
            jnp.where(group, jnp.where(lane - b == sub, F32(1), zero), a[0]),
            jnp.where(group, jnp.where(lane - b - SUB == sub, F32(1), zero), a[1]),
        ]
        pivots, taken = eliminate(col0, col1, [a, w], mine)
        emit(g, pivots, *taken)
        recips = 1.0 / pivots
        a0, w0 = a[0] * recips, w[0] * recips
        above = [lane_of(a0, b + SUB + k) for k in range(SUB)]
        a, w = [a[1]], [w[1]]
        pivots, taken = eliminate(col1[SUB:], None, [a, w], mine)
        emit(g + 1, pivots, *taken)

        left = lane < b + 2 * SUB
        solved1 = jnp.where(left, w[0], a[0]) * (1.0 / pivots)
        lower_rows = [row_of(solved1, k) for k in range(SUB)]
        solved0 = jnp.where(left, w0, a0) - total_of(c * r for c, r in zip(above, lower_rows))
        solved = [row_of(solved0, k) for k in range(SUB)] + lower_rows
        rows[g], rows[g + 1] = solved0, solved1
        for h in near:
            rows[h] = jnp.where(group, zero, rows[h]) - total_of(f * s for f, s in zip(factors[h], solved))
        far = g + 4
        if far < count:
            panel = jnp.concatenate([rows[h] if g <= h < g + 2 else zero for h in range(count)], axis=0)
            rest = jnp.concatenate(rows[far:], axis=0)
            lanes = lax.broadcasted_iota(jnp.int32, rest.shape, 1)
            in_group = (lanes >= b) & (lanes < b + 2 * SUB)
            rest = jnp.where(in_group, F32(0), rest) - product(left_parts(rest), right_parts(panel))
            for i in range(far, count):
                rows[i] = rest[SUB * (i - far) : SUB * (i - far + 1), :]


def at(i, size=NB):
    return slice(i * size, (i + 1) * size)


def apart(n):
    return [(i, j) for i in range(n) for j in range(i + 1, n)]


def triangle_masks():
    r = lax.broadcasted_iota(jnp.int32, (NB, NB), 0)
    c = lax.broadcasted_iota(jnp.int32, (NB, NB), 1)
    return r < c, r == c


def halves(bit, all_ref, keep_ref, send_ref):
    size = keep_ref.shape[0]
    keep_ref[...] = all_ref[pl.ds(pl.multiple_of(bit * size, SUB), size), :]
    send_ref[...] = all_ref[pl.ds(pl.multiple_of((1 - bit) * size, SUB), size), :]


def square_layout(n):
    packs, offs = n // 4, len(apart(n)) // 2
    place = {(i, i): ((i // 2) // packs, (i // 2) % packs) for i in range(n)}
    place.update({ij: (number // offs, packs + number % offs) for number, ij in enumerate(apart(n))})
    return place, packs + offs


def square_products(core, start, left_of, right, out_ref):
    n = right.shape[1] // NB
    place, tail = square_layout(n)
    above, on = triangle_masks()
    for i in range(n):
        mine = [j for j in range(i, n) if place[i, j][0] == core]
        if not mine:
            continue
        row = product(left_of(i), right[:, mine[0] * NB :])
        for j in mine:
            block = row[:, at(j - mine[0])]
            where = slice(start + place[i, j][1] * NB, start + (place[i, j][1] + 1) * NB)
            if i != j:
                out_ref[where, :] = block
            elif i % 2 == 0:
                even = block
            else:
                out_ref[where, :] = jnp.where(above | on, even, block)
                pivots = jnp.sum(jnp.where(on, block, F32(0)), axis=0, keepdims=True)
                row_at = start + tail * NB + place[i, j][1]
                out_ref[row_at : row_at + 1, :] = pivots


def square_blocks(ref, start, n):
    above, on = triangle_masks()
    place, tail = square_layout(n)

    def block(i, j):
        core, number = place[i, j]
        both = ref[core, start + number * NB : start + (number + 1) * NB, :]
        if i != j:
            return both
        if i % 2 == 0:
            return jnp.where(above | on, both, both.T)
        row_at = start + tail * NB + number
        return jnp.where(on, ref[core, row_at : row_at + 1, :], jnp.where(above, both.T, both))

    return block


def copy_kernel(x_ref, out_ref):
    out_ref[...] = x_ref[...]


def gram_first_kernel(s_ref, own_ref, other_ref, keep_ref, send_ref, all_ref):
    all_ref[...] = jnp.zeros_like(all_ref)
    for core, e_ref in ((0, own_ref), (1, other_ref)):

        @pl.when(s_ref[0] == core)
        def _():
            square_products(core, 0, lambda i: left_parts(e_ref[:, at(i)].T), right_parts(e_ref[...]), all_ref)

    halves(s_ref[1], all_ref, keep_ref, send_ref)


def gram_second_kernel(s_ref, own_ref, other_ref, keep_ref, send_ref, all_ref):
    width = own_ref.shape[1]
    half = width // 2
    per_row = half // NB
    behind = width // NB * per_row * NB
    all_ref[behind:, :] = jnp.zeros((all_ref.shape[0] - behind, NB), F32)
    for core, first_ref, second_ref in ((0, own_ref, other_ref), (1, other_ref, own_ref)):

        @pl.when(s_ref[0] == core)
        def _():
            right = right_parts(second_ref[...])
            for i in range(width // NB):
                row = product(left_parts(first_ref[:, at(i)].T), right[:, core * half : (core + 1) * half])
                for j in range(per_row):
                    all_ref[at(i * per_row + j), :] = row[:, at(j)]
            square_products(core, behind, lambda i: left_parts(second_ref[:, at(i)].T), right, all_ref)

    halves(s_ref[3], all_ref, keep_ref, send_ref)


def gather_halves(t, s_ref, bit, parts, out_ref):
    size = parts[0].shape[0]
    places = ((t, s_ref[bit]), (t, 1 - s_ref[bit]), (1 - t, s_ref[bit + 1]), (1 - t, 1 - s_ref[bit + 1]))
    for (core, which), ref in zip(places, parts):
        out_ref[core, pl.ds(pl.multiple_of(which * size, SUB), size), :] = ref[...]


def factor_step(k, n, read, upper_ref, inv_ref, write, pending):
    source = read(k, k) * F32(ROOT_SCALE**2)

    def put_upper(g, v):
        upper_ref[at(g, SUB), at(k)] = v * F32(1 / ROOT_SCALE)

    def put_inverse(g, v):
        inv_ref[at(g, SUB), :] = v * F32(ROOT_SCALE)

    factor_block([source[at(h, SUB), :] for h in range(NB // SUB)], put_upper, put_inverse, pending)
    if k:
        upper_ref[:, : k * NB] = jnp.zeros((NB, k * NB), F32)
    inverse = inv_ref[...]
    lowers, rights = {}, {}
    if k + 1 < n:
        inverse_left = left_parts(inverse)

        def upper_block(j):
            upper = product(inverse_left, right_parts(read(k, j)))
            lowers[j], rights[j] = column_parts(upper)
            upper_ref[:, at(j)] = upper

        def update(i, columns):
            change = product_of_columns(lowers[i], jnp.concatenate([rights[j] for j in columns], axis=1))
            for number, j in enumerate(columns):
                write(i, j, read(i, j) - change[:, at(number)])

        upper_block(k + 1)
        update(k + 1, [k + 1])
        pending += [functools.partial(upper_block, j) for j in range(k + 2, n)]
        if k + 2 < n:
            pending.append(functools.partial(update, k + 1, range(k + 2, n)))
        pending += [functools.partial(update, i, range(i, n)) for i in range(k + 2, n)]
    return inverse, lowers, rights


def invert_step(k, n, inverse, lowers, read, write, out_ref, left_ref, pending):
    right = []

    def own_row():
        left = left_parts(inverse)
        row = [product(left, right_parts(read(k, j))) for j in range(k)] + [inverse]
        for j, block in enumerate(row):
            out_ref[:, at(j)] = block
        if k + 1 < n:
            out_ref[:, (k + 1) * NB :] = jnp.zeros((NB, (n - k - 1) * NB), F32)
        row = jnp.concatenate(row, axis=1)
        right.append(right_parts(row))
        left_ref[...] = left_parts(row)

    def update(i):
        change = product_of_columns(lowers[i], right[0])
        for j in range(k + 1):
            write(i, j, (read(i, j) if j < k else F32(0)) - change[:, at(j)])

    pending.append(own_row)
    pending += [functools.partial(update, i) for i in range(k + 1, n)]


def solve_columns(first, own_ref, other_ref, row_refs, out_refs, start):
    def column(k, row_ref, out_ref):
        depth = (k + 1) * NB
        effects = jnp.where(first, own_ref[:, :depth], other_ref[:, :depth])
        out_ref[...] = product(left_parts(effects), right_parts(row_ref[:, :depth].T))

    return [functools.partial(column, k, *refs) for k, *refs in zip(range(start, start + len(row_refs)), row_refs, out_refs)]


def start_kernel(ks, s_ref, p0, p1, p2, p3, *refs):
    sums_ref = refs[-1]
    n = refs[0].shape[1] // NB
    gather_halves(s_ref[0], s_ref, 1, (p0, p1, p2, p3), sums_ref)
    row_steps(ks, n, square_blocks(sums_ref, 0, n), None, [], *refs[:-1])


def next_kernel(ks, before, s_ref, own_ref, other_ref, *refs):
    row_refs, (rest_in, inv_rest_in), refs = refs[: len(before)], refs[len(before) : len(before) + 2], refs[len(before) + 2 :]
    n = own_ref.shape[1] // NB
    pending = solve_columns(s_ref[0] == 0, own_ref, other_ref, row_refs, refs[: len(before)], before[0])

    def gram(i, j):
        return rest_in[at(i), at(j)]

    def inv_gram(i, j):
        return inv_rest_in[at(i), at(j)]

    row_steps(ks, n, gram, inv_gram, pending, *refs[len(before) :])


def row_steps(ks, n, gram, inv_gram, pending, *refs):
    rest_ref, inv_rest_ref, inv_ref = refs[3 * len(ks) :]

    def rest(i, j):
        return rest_ref[at(i), at(j)]

    def inv_rest(i, j):
        return inv_rest_ref[at(i), at(j)]

    for number, k in enumerate(ks):
        sources = (gram, inv_gram) if number == 0 else (rest, inv_rest)
        one_step(k, n, *sources, pending, *refs[number : 3 * len(ks) : len(ks)], rest_ref, inv_rest_ref, inv_ref)
    run_share(pending, 1)


def one_step(k, n, gram, inv_gram, pending, upper_ref, left_ref, row_ref, rest_ref, inv_rest_ref, inv_ref):
    def write(i, j, v):
        rest_ref[at(i), at(j)] = v

    def inv_write(i, j, v):
        inv_rest_ref[at(i), at(j)] = v

    inverse, lowers, _ = factor_step(k, n, gram, upper_ref, inv_ref, write, pending)
    invert_step(k, n, inverse, lowers, inv_gram, inv_write, row_ref, left_ref, pending)


def last_kernel(scale, s_ref, *refs):
    parts, (own_ref, other_ref), refs = refs[:4], refs[4:6], refs[6:]
    width = own_ref.shape[1]
    n = width // NB
    upper_refs, left_refs, first_refs, refs = refs[:n], refs[n : 2 * n], refs[2 * n : 3 * n - 1], refs[3 * n - 1 :]
    inv_row_ref, basis_ref, tri_ref, sums_ref, cross_upper_ref, work_ref, row_ref, e_ref, inv_ref, column_ref = refs
    t = s_ref[0]
    gather_halves(t, s_ref, 3, parts, sums_ref)
    gram = square_blocks(sums_ref, n * (n // 2) * NB, n)
    first = t == 0
    lowers, rights = {}, {}

    def cross_column(j):
        core, col = divmod(j, n // 2)
        parts = split(jnp.concatenate([sums_ref[core, at(i * (n // 2) + col), :] for i in range(n)], axis=0))
        column = []
        for k in range(n):
            h, m, l = (x[: (k + 1) * NB, :] for x in parts)
            column.append(product(left_refs[k][...], jnp.concatenate([h, m, h, m, l, h], axis=0)))
            cross_upper_ref[at(k), at(j)] = column[k]
        column = jnp.concatenate(column, axis=0)
        lowers[j], rights[j] = column_parts(column)

    def take_off(i, columns):
        change = product_of_columns(lowers[i], jnp.concatenate([rights[j] for j in columns], axis=1))
        for number, j in enumerate(columns):
            work_ref[at(i), at(j)] = gram(i, j) - change[:, at(number)]

    def take_off_effects():
        solved = jnp.concatenate([ref[...] for ref in (*first_refs, column_ref)], axis=1)
        effects = jnp.where(first, other_ref[...], own_ref[...])
        e_ref[...] = effects - product(left_parts(solved), jnp.concatenate([rights[j] for j in range(n)], axis=1))

    def upper_rows(k):
        tri_ref[at(k), :] = jnp.where(first, upper_refs[k][...], cross_upper_ref[at(k), :]) * (1.0 / scale)

    def solve_effects(k, inverse, rights):
        solved = product(left_parts(e_ref[:, at(k)]), right_parts(inverse.T))
        if k + 1 < n:
            later = jnp.concatenate([rights[j] for j in range(k + 1, n)], axis=1)
            e_ref[:, (k + 1) * NB :] -= product(left_parts(solved), later)
        done = first_refs[k] if k + 1 < n else column_ref
        basis_ref[:, at(k)] = jnp.where(first, done[...], solved) * scale
        tri_ref[at(n + k), :] = jnp.where(first, F32(0), row_ref[k % 2] * (1.0 / scale))

    def read(i, j):
        return work_ref[at(i), at(j)]

    def write(i, j, v):
        work_ref[at(i), at(j)] = v

    cross_column(0)
    take_off(0, [0])
    pending = [functools.partial(cross_column, j) for j in range(1, n)]
    pending.append(functools.partial(take_off, 0, range(1, n)))
    pending += [functools.partial(take_off, i, range(i, n)) for i in range(1, n)]
    pending += solve_columns(first, own_ref, other_ref, [inv_row_ref], [column_ref], n - 1)
    pending.append(take_off_effects)
    pending += [functools.partial(upper_rows, k) for k in range(n)]
    for k in range(n):
        inverse, _, row_rights = factor_step(k, n, read, row_ref.at[k % 2], inv_ref, write, pending)
        pending.append(functools.partial(solve_effects, k, inverse, row_rights))
    run_share(pending, 1)


def shards(n_rows, effects):
    rows, width = effects.shape
    cols = 2 * width
    half = width // NB
    t = lax.axis_index("tensor")
    me = lax.axis_index("rows")
    swap = [(0, 1), (1, 0)]

    steps = n_rows.bit_length() - 1
    straight = [1 << j for j in range(steps)]
    crossed = straight[1::-1] + straight[2:]

    def bit(masks, j, core):
        return jnp.where(core == 0, (me // masks[0][j]) % 2, (me // masks[1][j]) % 2)

    def exchange(x, masks, j):
        perm = [(2 * r + c, 2 * (r ^ masks[c][j]) + c) for r in range(n_rows) for c in range(2)]
        return lax.ppermute(x, ("rows", "tensor"), perm)

    def sum_rows(keep, send, masks):
        def tie(got, gate):
            return got if gate is None else lax.optimization_barrier((got, gate))[0]

        got = exchange(send, masks, 0)
        total = keep + tie(got, (yield keep))
        for j in range(1, steps - 1):
            piece = total.shape[0] // 2
            v = bit(masks, j, t)
            sent, total = (lax.dynamic_slice_in_dim(total, i * piece, piece) for i in (1 - v, v))
            got = exchange(sent, masks, j)
            total = total + tie(got, (yield total))
        got = exchange(total, masks, steps - 1)
        total = total + tie(got, (yield total))
        for j in range(steps - 2, 0, -1):
            got = exchange(total, masks, j)
            got = tie(got, (yield total))
            v = bit(masks, j, t)
            total = jnp.concatenate([jnp.where(v == 0, total, got), jnp.where(v == 0, got, total)])
        got = exchange(total, masks, 0)
        got = tie(got, (yield total))
        yield total, got, lax.ppermute(total, "tensor", swap), lax.ppermute(got, "tensor", swap)

    vmem = pl.BlockSpec(memory_space=pltpu.VMEM)
    smem = pl.BlockSpec(memory_space=pltpu.SMEM)
    params = pltpu.CompilerParams(vmem_limit_bytes=20 * 2**20)

    def array(*shape):
        return jax.ShapeDtypeStruct(shape, F32)

    def call(kernel, name, out_shape, scratch, *args):
        scalar = [a.dtype == jnp.int32 for a in args]
        return pl.pallas_call(
            kernel,
            out_shape=out_shape,
            in_specs=[smem if s else vmem for s in scalar],
            out_specs=tuple(vmem for _ in out_shape),
            scratch_shapes=[pltpu.VMEM(shape, F32) for shape in scratch],
            cost_estimate=pl.CostEstimate(flops=0, bytes_accessed=0, transcendentals=0),
            compiler_params=params,
            name=name,
        )(*args)

    first_masks, second_masks = (straight, crossed), (crossed, straight)
    scalars = jnp.stack([t] + [bit(m, 0, core) for m in (first_masks, second_masks) for core in (t, 1 - t)]).astype(jnp.int32)

    grain = SUB * max(n_rows // 2, 2)
    first_rows = square_layout(half)[1] * NB
    second_rows = first_rows + half * half // 2 * NB
    first_rows, second_rows = (x + -(-(half // 4) // grain) * grain for x in (first_rows, second_rows))

    other = lax.ppermute(effects, "tensor", swap)
    def halves_of(size):
        return (array(size // 2, NB),) * 2

    (own,) = call(copy_kernel, "own_copy", (array(rows, width),), [], effects)
    first = call(gram_first_kernel, "gram_first", halves_of(first_rows), [(first_rows, NB)], scalars, own, other)
    second = call(gram_second_kernel, "gram_second", halves_of(second_rows), [(second_rows, NB)], scalars, own, other)
    first_keep, *second = lax.optimization_barrier((first[0], *second))
    one, two = sum_rows(first_keep, first[1], first_masks), sum_rows(*second, second_masks)
    next(one), next(two)
    stages = 2 * steps - 1
    for i in range(stages):
        first_sums = one.send(None)
        if i >= 2:
            two.send(None)

    uppers, lefts, inverse_rows, solved = [], [], [], []
    rest = first_sums
    before = []
    for ks in ([0], list(range(1, half - 1)), [half - 1]):
        columns = [array(rows, NB) for _ in before]
        out = [array(NB, width) for _ in ks]
        out += [jax.ShapeDtypeStruct((NB, 6 * (k + 1) * NB), BF16) for k in ks]
        out += [array(NB, width) for _ in ks]
        final = ks[-1] == half - 1
        out += [] if final else [array(width, width), array(width, width)]
        if before:
            kernel, scratch = functools.partial(next_kernel, ks, before), ([(SUB, NB)] * 2 if final else []) + [(NB, NB)]
            args = (scalars, own, other, *inverse_rows[before[0] :], *rest)
        else:
            kernel, scratch = functools.partial(start_kernel, ks), [(NB, NB), (2, first_rows, NB)]
            args = (scalars, *rest)
        made = call(kernel, "factor_rows", columns + out, scratch, *args)
        rest = made[-2:]
        solved += made[: len(before)]
        made = made[len(before) :]
        for group, number in ((uppers, 0), (lefts, 1), (inverse_rows, 2)):
            group += made[number * len(ks) : (number + 1) * len(ks)]
        before = ks

    for gate in (uppers[0], uppers[-2]):
        second_sums = two.send(gate)
    scale = float(rows * n_rows) ** 0.5
    scratch = [(2, second_rows, NB), (width, width), (width, width), (2, NB, width), (rows, width), (NB, NB), (rows, NB)]
    return call(
        functools.partial(last_kernel, scale),
        "factor_last",
        (array(rows, width), array(cols, width)),
        scratch,
        *(scalars, *second_sums, own, other, *uppers, *lefts, *solved, *inverse_rows[before[0] :]),
    )


def solution(mesh):
    spec = P(("groups", "rows"), "tensor")
    return jax.shard_map(
        functools.partial(shards, mesh.shape["rows"]),
        mesh=mesh,
        in_specs=(spec,),
        out_specs=(spec, P("groups", "tensor")),
        check_vma=False,
    )
```
